512 devices in a mesh: shard: 128 (over y, z, core), grp: 4 (over x).
Axes of the slice: x: 4, y: 8, z: 8, core: 2. Of those that a mesh axis runs over, the one named last changes fastest.
Arguments:
- embeddings: bfloat16 [262144, 768], P(('shard', 'grp')), may hold values from -18 to 18
- cluster_id: int32 [262144], P(('shard', 'grp')), may hold values from 0 to 1001
- row_targets: int32 [262144, 3], P(('shard', 'grp')), may hold values from -1 to 511, as said below
Outputs:
- nearest_similarity: float32 [262144], P(('shard', 'grp'))
The draws below stay inside these ranges and needn't reach their ends.
Inputs may be any that keep to these rules, and one draw needn't show every extreme that they name: `row_targets`: each row names 1 to 3 distinct devices and -1 in its other entries. Among the rows of one device at most 2 entries name one device, and some device is named by exactly 2 entries of every device's rows.
All inputs are finite; a program needn't handle non-finite values.
Results may differ from the reference program's by a relative error of at most 0.00069.
Values may be sent and summed in bfloat16 or wider, within the bound.
A program may use at most 64 MiB of HBM per device.

```python
import jax
import jax.numpy as jnp
import numpy as np
from jax import lax

D = 768
BUCKET = 1024
GIANTS = 2
CPO = 2
ROWS_DEV = 512
CAP = 2
COPIES = 3
CLUSTERS = 1002
ROWS = 262144
DEVICES = 512


pair_table = np.array([[0, 1, 2], [0, 3, 4], [1, 3, 5], [2, 4, 5]], dtype=np.int32)


def cluster_plan(key):
    owners_count = DEVICES - 6 * GIANTS
    half = CAP // 2
    owner_units = owners_count * CAP
    giant_units = 4 * half
    units = owner_units + GIANTS * giant_units
    roles = jax.random.permutation(jax.random.fold_in(key, 21), DEVICES).astype(jnp.int32)
    helpers = roles[:6 * GIANTS]
    owners = roles[6 * GIANTS:]
    heavy = jax.random.randint(jax.random.fold_in(key, 22), (), 0, owners_count)
    device_keys = jax.random.split(jax.random.fold_in(key, 23), DEVICES)
    lookup = jnp.asarray(pair_table)

    def one_device(device_key):
        first_key, second_key, third_key = jax.random.split(device_key, 3)
        unit_ids = jnp.arange(units, dtype=jnp.int32)
        ranking = jax.random.permutation(first_key, units).astype(jnp.int32)
        forced = (unit_ids < owner_units) & (unit_ids // CAP == heavy) | (unit_ids >= owner_units) & (unit_ids < owner_units + giant_units)
        ranking = jnp.where(forced, -1, ranking)
        chosen = jnp.argsort(ranking, stable=True)[:ROWS_DEV].astype(jnp.int32)
        chosen = jax.random.permutation(second_key, chosen)
        extra = jax.random.randint(third_key, (ROWS_DEV,), 0, CPO).astype(jnp.int32)
        drawn = chosen < owner_units
        owner_index = jnp.clip(chosen // CAP, 0, owners_count - 1)
        giant_offset = jnp.maximum(chosen - owner_units, 0)
        giant_index = jnp.clip(giant_offset // giant_units, 0, GIANTS - 1)
        block_index = giant_offset % giant_units // half
        clusters = jnp.where(drawn, owner_index * CPO + extra, owners_count * CPO + giant_index)
        giant_targets = helpers[giant_index[:, None] * 6 + lookup[block_index]]
        lone = jnp.full((ROWS_DEV, COPIES - 1), -1, jnp.int32)
        drawn_targets = jnp.concatenate([owners[owner_index][:, None], lone], axis=1)
        targets = jnp.where(drawn[:, None], drawn_targets, giant_targets)
        return (clusters.astype(jnp.int32), targets.astype(jnp.int32))
    clusters, targets = jax.vmap(one_device)(device_keys)
    return (clusters.reshape(-1), targets.reshape(-1, COPIES))


def draw_cluster_id(key, part):
    clusters, targets = cluster_plan(key)
    return clusters


def draw_row_targets(key, part):
    clusters, targets = cluster_plan(key)
    return targets


def draw_embeddings(key, part):
    clusters, targets = cluster_plan(key)
    key = jax.random.fold_in(key, 5)
    center_key, spread_key, noise_key = jax.random.split(key, 3)
    centers = jnp.clip(jax.random.normal(center_key, (CLUSTERS, D), jnp.float32), -5.0, 5.0)
    spreads = jnp.exp(jax.random.uniform(spread_key, (CLUSTERS,), jnp.float32, jnp.log(0.4), jnp.log(2.5)))
    noise = jnp.clip(jax.random.normal(noise_key, (ROWS, D), jnp.float32), -5.0, 5.0)
    values = centers[clusters] + spreads[clusters][:, None] * noise
    return values.astype(jnp.bfloat16)


def setup_inputs(seed: int = 0) -> dict:
    keys = jax.random.split(jax.random.key(seed), 4)
    return {
        "embeddings": draw_embeddings(jax.random.fold_in(keys[3], 71), 0),
        "cluster_id": draw_cluster_id(jax.random.fold_in(keys[3], 71), 0),
        "row_targets": draw_row_targets(jax.random.fold_in(keys[3], 71), 0),
    }


def slot_places(targets):
    count = targets.shape[0]
    keyed = jnp.where(targets >= 0, targets, DEVICES).astype(jnp.int32)
    order = jnp.argsort(keyed, stable=True).astype(jnp.int32)
    ordered = keyed[order]
    positions = jnp.arange(count, dtype=jnp.int32)
    fresh = jnp.concatenate([jnp.ones((1,), jnp.bool_), ordered[1:] != ordered[:-1]])
    first = lax.cummax(jnp.where(fresh, positions, 0).astype(jnp.int32), axis=0)
    ranks = jnp.zeros((count,), jnp.int32).at[order].set((positions - first).astype(jnp.int32))
    return jnp.where(targets >= 0, targets * CAP + ranks, -1).astype(jnp.int32)

def reference(embeddings, cluster_id, row_targets):
    values = embeddings.astype(jnp.float32)
    squares = lax.optimization_barrier(jnp.sum(values * values, axis=1, keepdims=True))
    unit = (values * lax.rsqrt(squares + 1e-06)).astype(jnp.bfloat16)
    places = jax.vmap(slot_places)(row_targets.reshape(DEVICES, ROWS_DEV * COPIES))
    source = jnp.arange(DEVICES, dtype=jnp.int32)[:, None]
    row_number = (source * ROWS_DEV + jnp.arange(ROWS_DEV * COPIES, dtype=jnp.int32)[None, :] // COPIES).astype(jnp.int32)
    table_index = places // CAP * BUCKET + source * CAP + places % CAP
    table_index = jnp.where(places >= 0, table_index, DEVICES * BUCKET).astype(jnp.int32)
    table = jnp.full((DEVICES * BUCKET,), -1, jnp.int32).at[table_index.reshape(-1)].set(row_number.reshape(-1), mode='drop')
    table = table.reshape(DEVICES, BUCKET)
    diagonal = jnp.arange(BUCKET, dtype=jnp.int32)[:, None] == jnp.arange(BUCKET, dtype=jnp.int32)[None, :]

    def per_bucket(members):
        filled = members >= 0
        picked = jnp.maximum(members, 0).astype(jnp.int32)
        member_rows = unit[picked].astype(jnp.float32)
        member_tags = jnp.where(filled, cluster_id[picked], -1).astype(jnp.int32)
        scores = jnp.dot(member_rows, member_rows.T, precision=lax.Precision.HIGHEST, preferred_element_type=jnp.float32)
        allowed = (member_tags[:, None] == member_tags[None, :]) & (member_tags[:, None] >= 0) & (member_tags[None, :] >= 0) & ~diagonal
        return lax.optimization_barrier(jnp.max(jnp.where(allowed, scores, jnp.float32(-1.0)), axis=1))
    maxima = lax.map(per_bucket, table).reshape(-1)
    found = jnp.where(places >= 0, maxima[jnp.minimum(table_index, DEVICES * BUCKET - 1)], jnp.float32(-1.0))
    return lax.optimization_barrier(jnp.max(found.reshape(DEVICES, ROWS_DEV, COPIES), axis=2)).reshape(ROWS)
```

```python
import jax
import jax.numpy as jnp
from jax import lax
from jax.experimental import pallas as pl
from jax.experimental.pallas import tpu as pltpu
from jax.sharding import PartitionSpec as P

MESH = pl.DeviceIdType.MESH
SIDE = 8
CORES = 2
SHARDS = SIDE * SIDE * CORES
GROUPS = 4
CAP = 2
PAIR = GROUPS * CAP
LANES = 128
CHUNK = 16
CHUNKS = SHARDS // CHUNK
ORDER = (4, 5, 0, 1, 2, 3, 6, 7)
EARLY = 2
TAGS_AFTER = 3
TURNS_AFTER = (4, 5)
SCORES_AFTER = (6, 7)
SCORED = (0, 32, 64, 96, 112, 128)


def sway(n):
    return (n + 1) // 2 * (n % 2 * 2 - 1) % SIDE


def steps(place):
    half = SIDE // 2
    chunk, pair, odd = place // CHUNK, place % CHUNK // 2, place % 2
    first = (chunk // CORES == 0) * 1
    sign = 1 - 2 * odd
    near, far = pair % half, pair // half
    dy = first * (sign * near + half * odd * ((near == 0) * 1)) + (1 - first) * sign * sway(pair)
    dz = dy + first * half * far + (1 - first) * sign * (chunk // CORES)
    return (dy + SIDE) % SIDE, (dz + 2 * SIDE) % SIDE, chunk % CORES


def shard_at(me, place, sign):
    dy, dz, dc = steps(place)
    y = (me // (SIDE * CORES) + sign * dy + SIDE) % SIDE
    z = ((me // CORES) % SIDE + sign * dz + SIDE) % SIDE
    c = (me + dc) % CORES
    return (y * SIDE + z) * CORES + c


def kernel(
    emb_hbm,
    cid_hbm,
    tgt_hbm,
    out_ref,
    emb_ref,
    cid_ref,
    tgt_ref,
    unit,
    hot,
    xsend,
    stage,
    ysend,
    recv,
    mid,
    tiles,
    tag_xs,
    ret_xs,
    tag_send,
    tag_recv,
    ret_send,
    ret_recv,
    peak,
    in_sem,
    xs_sem,
    xr_sem,
    ys_sem,
    yr_sem,
    tile_ss,
    tile_rs,
    row_ss,
    row_rs,
):
    rows, features = emb_ref.shape
    me = lax.axis_index("shard")
    grp = lax.axis_index("grp")
    f32 = jnp.float32
    bf16 = jnp.bfloat16

    incoming = [
        pltpu.make_async_copy(src, dst, in_sem.at[n])
        for n, (src, dst) in enumerate(
            [(tgt_hbm, tgt_ref), (cid_hbm, cid_ref), (emb_hbm, emb_ref)]
        )
    ]
    for copy in incoming:
        copy.start()

    ys = [(me // (SIDE * CORES) + d) % SIDE * (SIDE * CORES) for d in range(SIDE)]
    zs = [(me // CORES + d) % SIDE * CORES for d in range(SIDE)]
    cs = [(me + d) % CORES for d in range(CORES)]

    def at(dy, dz, dc):
        return {"shard": ys[dy % SIDE] + zs[dz % SIDE] + cs[dc]}

    def ahead(place):
        return at(*steps(place))

    def behind(place):
        dy, dz, dc = steps(place)
        return at(-dy, -dz, dc)

    def along(e):
        return {"grp": (grp + e + GROUPS) % GROUPS}

    barrier = pltpu.get_barrier_semaphore()
    for e in range(1, GROUPS):
        pl.semaphore_signal(
            barrier, inc=1, device_id=along(e), device_id_type=MESH
        )
    for place in range(1, SHARDS):
        pl.semaphore_signal(barrier, inc=1, device_id=ahead(place), device_id_type=MESH)

    place = lax.broadcasted_iota(jnp.int32, (SHARDS, 1), 0)
    peers = shard_at(me, place, 1) * GROUPS
    before = lax.broadcasted_iota(jnp.int32, (rows, rows), 0) < lax.broadcasted_iota(
        jnp.int32, (rows, rows), 1
    )
    before = jnp.where(before, 1.0, 0.0).astype(bf16)
    incoming[0].wait()
    named = []
    for e in range(GROUPS):
        target = peers + (grp + e) % GROUPS
        hit = tgt_ref[0:1, :] == target
        for c in range(1, tgt_ref.shape[0]):
            hit = hit | (tgt_ref[c : c + 1, :] == target)
        named.append(jnp.where(hit, 1.0, 0.0).astype(f32))
    named = jnp.concatenate(named, axis=0)
    rank = jnp.dot(named.astype(bf16), before, preferred_element_type=f32)
    for r in range(CAP):
        pick = jnp.where(rank == float(r), named, 0.0).astype(bf16)
        for e in range(GROUPS):
            hot[e * CAP + r] = pick[e * SHARDS : (e + 1) * SHARDS, :]

    incoming[2].wait()
    values = emb_ref[...].astype(f32)
    squares = jnp.sum(values * values, axis=1, keepdims=True)
    unit[...] = (values * lax.rsqrt(squares + 1e-06)).astype(bf16)

    size = PAIR * CHUNK
    order_out = lax.broadcasted_iota(jnp.int32, (size, size), 0)
    order_in = lax.broadcasted_iota(jnp.int32, (size, size), 1)
    turn = (order_in % CHUNK == order_out // PAIR) & (order_in // CHUNK == order_out % PAIR)
    turn = jnp.where(turn, 1.0, 0.0).astype(bf16)
    back = (order_out % CHUNK == order_in // PAIR) & (order_out // CHUNK == order_in % PAIR)
    back = jnp.where(back, 1.0, 0.0).astype(bf16)

    def by_place_first(block):
        block = jnp.dot(turn, block, preferred_element_type=f32).astype(bf16)
        return block.reshape(CHUNK, PAIR, features)

    def keep_for_x(k, j, block):
        e, r = j // CAP, j % CAP
        if e == 0:
            stage[k, 0, r * CHUNK : (r + 1) * CHUNK, :] = block
        else:
            xsend[k, e - 1, r * CHUNK : (r + 1) * CHUNK, :] = block

    def pack_rows(chunks):
        pick = [hot[j, k * CHUNK : (k + 1) * CHUNK, :] for k in chunks for j in range(PAIR)]
        packed = jnp.dot(
            jnp.concatenate(pick, axis=0), unit[...], preferred_element_type=f32
        ).astype(bf16)
        for n, k in enumerate(chunks):
            block = packed[n * size : (n + 1) * size, :]
            if k in ORDER[:EARLY]:
                ysend[k * CHUNK : (k + 1) * CHUNK] = by_place_first(block)
            else:
                for j in range(PAIR):
                    keep_for_x(k, j, block[j * CHUNK : (j + 1) * CHUNK, :])

    def x_copies(k):
        return [
            pltpu.make_async_remote_copy(
                src_ref=xsend.at[k, e - 1, pl.ds(r * CHUNK, CHUNK)],
                dst_ref=stage.at[k, e, pl.ds(r * CHUNK, CHUNK)],
                send_sem=xs_sem,
                recv_sem=xr_sem.at[k],
                device_id=along(e),
                device_id_type=MESH,
            )
            for r in range(CAP)
            for e in (1, 3, 2)
        ]

    def x_arrived(k):
        part = stage.at[k, pl.ds(1, GROUPS - 1)]
        pltpu.make_async_copy(part, part, xr_sem.at[k]).wait()
        return by_place_first(stage[k].reshape(size, features))

    def yz_arrived(k):
        first = max(1, k * CHUNK)
        part = pl.ds(first, (k + 1) * CHUNK - first)
        part = (mid if k in ORDER[:EARLY] else recv).at[part]
        pltpu.make_async_copy(part, part, yr_sem.at[k]).wait()

    def send_rows(n):
        k = ORDER[n]
        copies = [
            pltpu.make_async_remote_copy(
                src_ref=ysend.at[place],
                dst_ref=(mid if k in ORDER[:EARLY] else recv).at[place],
                send_sem=ys_sem,
                recv_sem=yr_sem.at[k],
                device_id=ahead(place),
                device_id_type=MESH,
            )
            for place in range(max(1, k * CHUNK), (k + 1) * CHUNK)
        ]
        if n + EARLY < CHUNKS:
            between = x_copies(ORDER[n + EARLY])
            for m, copy in enumerate(between):
                copies.insert(m + (m + 1) * CHUNK // (len(between) + 1), copy)
        for copy in copies:
            copy.start()

    def pass_rows(n):
        k = ORDER[n]
        ysend[k * CHUNK : (k + 1) * CHUNK] = x_arrived(k)
        if k == 0:
            recv[0] = ysend[0]
        send_rows(n)

    def turn_rows(k):
        yz_arrived(k)
        block = mid[k * CHUNK : (k + 1) * CHUNK].reshape(size, features)
        block = jnp.dot(back, block, preferred_element_type=f32).astype(bf16)
        for j in range(PAIR):
            keep_for_x(k, j, block[j * CHUNK : (j + 1) * CHUNK, :])
        for copy in x_copies(k):
            copy.start()

    pack_rows(ORDER[: 2 * EARLY])
    pl.semaphore_wait(barrier, SHARDS - 1 + GROUPS - 1)
    for n in range(EARLY):
        send_rows(n)
    pack_rows(ORDER[2 * EARLY :])

    row8 = lax.broadcasted_iota(jnp.int32, (PAIR, LANES), 0) // CAP

    def spread_tile(n, held, sign):
        for e in range(1, GROUPS):
            pltpu.make_async_remote_copy(
                src_ref=tiles.at[n],
                dst_ref=held.at[e - 1],
                send_sem=tile_ss.at[n],
                recv_sem=tile_rs.at[n],
                device_id=along(sign * e),
                device_id_type=MESH,
            ).start()

    def merge_tile(n, held):
        pltpu.make_async_copy(held, held, tile_rs.at[n]).wait()
        merged = tiles[n]
        for e in range(1, GROUPS):
            merged = jnp.where(row8 == e, held[e - 1], merged)
        return jnp.transpose(
            jnp.concatenate([merged, jnp.zeros((LANES - PAIR, LANES), f32)], axis=0)
        )

    others = pl.ds(1, SHARDS - 1)

    def spread_rows(n, sent, held, device):
        held[0] = sent[0]
        for place in range(1, SHARDS):
            pltpu.make_async_remote_copy(
                src_ref=sent.at[place],
                dst_ref=held.at[place],
                send_sem=row_ss.at[n],
                recv_sem=row_rs.at[n],
                device_id=device(place),
                device_id_type=MESH,
            ).start()

    def rows_arrived(n, held):
        pltpu.make_async_copy(held.at[others], held.at[others], row_rs.at[n]).wait()

    incoming[1].wait()
    cid = cid_ref[...].astype(f32) + 1.0
    lane = lax.broadcasted_iota(jnp.int32, (SHARDS, LANES), 1)
    tags = jnp.zeros((SHARDS, LANES), f32)
    for j in range(PAIR):
        tag = jnp.sum(hot[j].astype(f32) * cid, axis=1, keepdims=True)
        tags = jnp.where(lane == j, tag, tags)
    tiles[0] = jnp.transpose(tags)[0:PAIR, :] - 1.0
    spread_tile(0, tag_xs, 1)

    total = SHARDS * PAIR
    lanes = lax.broadcasted_iota(jnp.int32, (total, LANES), 1)
    member = lax.broadcasted_iota(jnp.int32, (total, LANES), 0)
    mine = lanes == member % PAIR
    number = lax.broadcasted_iota(jnp.int32, (total, 1), 0)
    column = lax.broadcasted_iota(jnp.int32, (1, total), 1)

    def member_tags():
        rows_arrived(0, tag_recv)
        spread = jnp.broadcast_to(tag_recv[...], (SHARDS, PAIR, LANES)).reshape(total, LANES)
        tag_col = jnp.sum(jnp.where(mine, spread, 0.0), axis=1, keepdims=True)
        tag_col = jnp.where(tag_col < 0.0, -2.0 - number.astype(f32), tag_col)
        return tag_col, jnp.transpose(jnp.broadcast_to(tag_col, (total, LANES)))[0:1, :]

    def fold(scores):
        best = scores[:, 0:LANES]
        for first in range(LANES, scores.shape[1], LANES):
            best = jnp.maximum(best, scores[:, first : first + LANES])
        return best

    def score(begin, end):
        for k in range(begin // CHUNK, end // CHUNK):
            if k in ORDER[:EARLY]:
                recv[k * CHUNK : (k + 1) * CHUNK] = x_arrived(k)
            else:
                yz_arrived(k)
        low, high = begin * PAIR, end * PAIR
        scores = lax.dot_general(
            recv[0:end].reshape(high, features),
            recv[begin:end].reshape(high - low, features),
            (((1,), (1,)), ((), ())),
            preferred_element_type=f32,
        )
        scores = jnp.where(tag_col[0:high, :] == tag_row[:, low:high], scores, -1.0)
        own = scores[low:high, :]
        own = fold(jnp.where(number[low:high, :] != column[:, low:high], own, -1.0))
        if low:
            past = scores[0:low, :]
            peak[0:low, :] = jnp.maximum(peak[0:low, :], fold(past))
            past = jnp.max(past, axis=0, keepdims=True)
            past = jnp.transpose(jnp.broadcast_to(past, (LANES, high - low)))
            own = jnp.maximum(own, past)
        peak[low:high, :] = own

    steps_left = list(zip(SCORED[:-1], SCORED[1:]))
    for n in range(EARLY, CHUNKS):
        pass_rows(n)
        if n == TAGS_AFTER:
            tag_send[...] = merge_tile(0, tag_xs).reshape(SHARDS, 1, LANES)
            spread_rows(0, tag_send, tag_recv, ahead)
        if n in TURNS_AFTER:
            turn_rows(ORDER[TURNS_AFTER.index(n)])
        if n in SCORES_AFTER:
            if n == SCORES_AFTER[0]:
                tag_col, tag_row = member_tags()
            score(*steps_left.pop(0))
    for begin, end in steps_left:
        score(begin, end)
    best = jnp.max(peak[...], axis=1, keepdims=True)
    best = jnp.where(mine, best, -2.0)
    ret_send[...] = jnp.max(best.reshape(SHARDS, PAIR, LANES), axis=1, keepdims=True)

    spread_rows(1, ret_send, ret_recv, behind)
    rows_arrived(1, ret_recv)
    tiles[1] = jnp.transpose(ret_recv[...].reshape(SHARDS, LANES))[0:PAIR, :]
    spread_tile(1, ret_xs, -1)
    final = merge_tile(1, ret_xs)
    found = jnp.full((SHARDS, rows), -1.0, f32)
    for j in range(PAIR):
        found = jnp.maximum(found, jnp.where(hot[j] > 0.5, final[:, j : j + 1], -1.0))
    out_ref[...] = jnp.max(found, axis=0, keepdims=True)

    pltpu.make_async_copy(xsend, xsend, xs_sem).wait()
    pltpu.make_async_copy(ysend.at[others], ysend.at[others], ys_sem).wait()
    for n, held in enumerate((tag_xs, ret_xs)):
        pltpu.make_async_copy(held, held, tile_ss.at[n]).wait()
    for n, sent in enumerate((tag_send, ret_send)):
        pltpu.make_async_copy(sent.at[others], sent.at[others], row_ss.at[n]).wait()


def body(embeddings, cluster_id, row_targets):
    rows = embeddings.shape[0]
    features = embeddings.shape[1]
    copies = row_targets.shape[1]
    f32, bf16 = jnp.float32, jnp.bfloat16
    dma = pltpu.SemaphoreType.DMA

    def held(count):
        return pltpu.VMEM((count, PAIR, LANES), f32)

    small = pltpu.VMEM((SHARDS, 1, LANES), f32)

    out = pl.pallas_call(
        kernel,
        out_shape=jax.ShapeDtypeStruct((1, rows), f32),
        in_specs=[pl.BlockSpec(memory_space=pltpu.HBM)] * 3,
        out_specs=pl.BlockSpec(memory_space=pltpu.VMEM),
        scratch_shapes=[
            pltpu.VMEM((rows, features), bf16),
            pltpu.VMEM((1, rows), jnp.int32),
            pltpu.VMEM((copies, rows), jnp.int32),
            pltpu.VMEM((rows, features), bf16),
            pltpu.VMEM((PAIR, SHARDS, rows), bf16),
            pltpu.VMEM((CHUNKS, GROUPS - 1, CAP * CHUNK, features), bf16),
            pltpu.VMEM((CHUNKS, GROUPS, CAP * CHUNK, features), bf16),
            pltpu.VMEM((SHARDS, PAIR, features), bf16),
            pltpu.VMEM((SHARDS, PAIR, features), bf16),
            pltpu.VMEM((SHARDS, PAIR, features), bf16),
            held(2),
            held(GROUPS - 1),
            held(GROUPS - 1),
            small,
            small,
            small,
            small,
            pltpu.VMEM((SHARDS * PAIR, LANES), f32),
            dma((3,)),
            dma,
            dma((CHUNKS,)),
            dma,
            dma((CHUNKS,)),
            dma((2,)),
            dma((2,)),
            dma((2,)),
            dma((2,)),
        ],
        compiler_params=pltpu.CompilerParams(
            collective_id=0, has_side_effects=True, vmem_limit_bytes=63 * 2**20
        ),
        name="dedup",
    )(embeddings, cluster_id.reshape(1, rows), row_targets.T)
    return out.reshape(rows)


def solution(mesh):
    placed = (P(("shard", "grp"), None), P(("shard", "grp")), P(("shard", "grp"), None))
    return jax.shard_map(
        body, mesh=mesh, in_specs=placed, out_specs=P(("shard", "grp")), check_vma=False
    )
```

```python
import jax
import jax.numpy as jnp
from jax import lax
from jax.experimental import pallas as pl
from jax.experimental.pallas import tpu as pltpu
from jax.sharding import PartitionSpec as P

MESH = pl.DeviceIdType.MESH
SIDE = 8
CORES = 2
SHARDS = SIDE * SIDE * CORES
GROUPS = 4
CAP = 2
PAIR = GROUPS * CAP
LANES = 128
PLANE = SHARDS // CORES
LINES = GROUPS * CORES
CHUNK = 16
CHUNKS = SHARDS // CHUNK
ORDER = (4, 5, 0, 1, 2, 3, 6, 7)
EARLY = 2
TAGS_AFTER = 3
TURNS_AFTER = (4, 5)
SCORES_AFTER = (6, 7)
SCORED = (0, 32, 64, 96, 112, 128)


def sway(n):
    return (n + 1) // 2 * (n % 2 * 2 - 1) % SIDE


def steps(place):
    half = SIDE // 2
    chunk, pair, odd = place // CHUNK, place % CHUNK // 2, place % 2
    first = (chunk // CORES == 0) * 1
    sign = 1 - 2 * odd
    near, far = pair % half, pair // half
    dy = first * (sign * near + half * odd * ((near == 0) * 1)) + (1 - first) * sign * sway(pair)
    dz = dy + first * half * far + (1 - first) * sign * (chunk // CORES)
    return (dy + SIDE) % SIDE, (dz + 2 * SIDE) % SIDE, chunk % CORES


def shard_at(me, place, sign):
    dy, dz, dc = steps(place)
    y = (me // (SIDE * CORES) + sign * dy + SIDE) % SIDE
    z = ((me // CORES) % SIDE + sign * dz + SIDE) % SIDE
    c = (me + dc) % CORES
    return (y * SIDE + z) * CORES + c


def kernel(
    emb_hbm,
    cid_hbm,
    tgt_hbm,
    out_ref,
    emb_ref,
    cid_ref,
    tgt_ref,
    unit,
    hot,
    xsend,
    stage,
    ysend,
    recv,
    mid,
    tiles,
    tag_xs,
    ret_xs,
    tag_send,
    tag_recv,
    ret_send,
    ret_recv,
    peak,
    in_sem,
    xs_sem,
    xr_sem,
    ys_sem,
    yr_sem,
    tile_ss,
    tile_rs,
    row_ss,
    row_rs,
):
    rows, features = emb_ref.shape
    me = lax.axis_index("shard")
    grp = lax.axis_index("grp")
    f32 = jnp.float32
    bf16 = jnp.bfloat16

    incoming = [
        pltpu.make_async_copy(src, dst, in_sem.at[n])
        for n, (src, dst) in enumerate(
            [(tgt_hbm, tgt_ref), (cid_hbm, cid_ref), (emb_hbm, emb_ref)]
        )
    ]
    for copy in incoming:
        copy.start()

    ys = [(me // (SIDE * CORES) + d) % SIDE * (SIDE * CORES) for d in range(SIDE)]
    zs = [(me // CORES + d) % SIDE * CORES for d in range(SIDE)]
    cs = [(me + d) % CORES for d in range(CORES)]

    def at(dy, dz, dc):
        return {"shard": ys[dy % SIDE] + zs[dz % SIDE] + cs[dc]}

    def ahead(place):
        return at(*steps(place))

    def along(e, dc=0):
        return {"shard": ys[0] + zs[0] + cs[dc], "grp": (grp + e + GROUPS) % GROUPS}

    barrier = pltpu.get_barrier_semaphore()
    for e in range(1, GROUPS):
        for dc in range(CORES):
            pl.semaphore_signal(barrier, inc=1, device_id=along(e, dc), device_id_type=MESH)
    for place in range(1, SHARDS):
        pl.semaphore_signal(barrier, inc=1, device_id=ahead(place), device_id_type=MESH)

    place = lax.broadcasted_iota(jnp.int32, (SHARDS, 1), 0)
    peers = shard_at(me, place, 1) * GROUPS
    before = lax.broadcasted_iota(jnp.int32, (rows, rows), 0) < lax.broadcasted_iota(
        jnp.int32, (rows, rows), 1
    )
    before = jnp.where(before, 1.0, 0.0).astype(bf16)
    incoming[0].wait()
    named = []
    for e in range(GROUPS):
        target = peers + (grp + e) % GROUPS
        hit = tgt_ref[0:1, :] == target
        for c in range(1, tgt_ref.shape[0]):
            hit = hit | (tgt_ref[c : c + 1, :] == target)
        named.append(jnp.where(hit, 1.0, 0.0).astype(f32))
    named = jnp.concatenate(named, axis=0)
    rank = jnp.dot(named.astype(bf16), before, preferred_element_type=f32)
    for r in range(CAP):
        pick = jnp.where(rank == float(r), named, 0.0).astype(bf16)
        for e in range(GROUPS):
            hot[e * CAP + r] = pick[e * SHARDS : (e + 1) * SHARDS, :]

    incoming[2].wait()
    values = emb_ref[...].astype(f32)
    squares = jnp.sum(values * values, axis=1, keepdims=True)
    unit[...] = (values * lax.rsqrt(squares + 1e-06)).astype(bf16)

    size = PAIR * CHUNK
    order_out = lax.broadcasted_iota(jnp.int32, (size, size), 0)
    order_in = lax.broadcasted_iota(jnp.int32, (size, size), 1)
    turn = (order_in % CHUNK == order_out // PAIR) & (order_in // CHUNK == order_out % PAIR)
    turn = jnp.where(turn, 1.0, 0.0).astype(bf16)
    back = (order_out % CHUNK == order_in // PAIR) & (order_out // CHUNK == order_in % PAIR)
    back = jnp.where(back, 1.0, 0.0).astype(bf16)

    def by_place_first(block):
        block = jnp.dot(turn, block, preferred_element_type=f32).astype(bf16)
        return block.reshape(CHUNK, PAIR, features)

    def keep_for_x(k, j, block):
        e, r = j // CAP, j % CAP
        if e == 0:
            stage[k, 0, r * CHUNK : (r + 1) * CHUNK, :] = block
        else:
            xsend[k, e - 1, r * CHUNK : (r + 1) * CHUNK, :] = block

    def pack_rows(chunks):
        pick = [hot[j, k * CHUNK : (k + 1) * CHUNK, :] for k in chunks for j in range(PAIR)]
        packed = jnp.dot(
            jnp.concatenate(pick, axis=0), unit[...], preferred_element_type=f32
        ).astype(bf16)
        for n, k in enumerate(chunks):
            block = packed[n * size : (n + 1) * size, :]
            if k in ORDER[:EARLY]:
                ysend[k * CHUNK : (k + 1) * CHUNK] = by_place_first(block)
            else:
                for j in range(PAIR):
                    keep_for_x(k, j, block[j * CHUNK : (j + 1) * CHUNK, :])

    def x_copies(k):
        return [
            pltpu.make_async_remote_copy(
                src_ref=xsend.at[k, e - 1, pl.ds(r * CHUNK, CHUNK)],
                dst_ref=stage.at[k, e, pl.ds(r * CHUNK, CHUNK)],
                send_sem=xs_sem,
                recv_sem=xr_sem.at[k],
                device_id=along(e),
                device_id_type=MESH,
            )
            for r in range(CAP)
            for e in (1, 3, 2)
        ]

    def x_arrived(k):
        part = stage.at[k, pl.ds(1, GROUPS - 1)]
        pltpu.make_async_copy(part, part, xr_sem.at[k]).wait()
        return by_place_first(stage[k].reshape(size, features))

    def yz_arrived(k):
        first = max(1, k * CHUNK)
        part = pl.ds(first, (k + 1) * CHUNK - first)
        part = (mid if k in ORDER[:EARLY] else recv).at[part]
        pltpu.make_async_copy(part, part, yr_sem.at[k]).wait()

    def send_rows(n):
        k = ORDER[n]
        copies = [
            pltpu.make_async_remote_copy(
                src_ref=ysend.at[place],
                dst_ref=(mid if k in ORDER[:EARLY] else recv).at[place],
                send_sem=ys_sem,
                recv_sem=yr_sem.at[k],
                device_id=ahead(place),
                device_id_type=MESH,
            )
            for place in range(max(1, k * CHUNK), (k + 1) * CHUNK)
        ]
        if n + EARLY < CHUNKS:
            between = x_copies(ORDER[n + EARLY])
            for m, copy in enumerate(between):
                copies.insert(m + (m + 1) * CHUNK // (len(between) + 1), copy)
        for copy in copies:
            copy.start()

    def pass_rows(n):
        k = ORDER[n]
        ysend[k * CHUNK : (k + 1) * CHUNK] = x_arrived(k)
        if k == 0:
            recv[0] = ysend[0]
        send_rows(n)

    def turn_rows(k):
        yz_arrived(k)
        block = mid[k * CHUNK : (k + 1) * CHUNK].reshape(size, features)
        block = jnp.dot(back, block, preferred_element_type=f32).astype(bf16)
        for j in range(PAIR):
            keep_for_x(k, j, block[j * CHUNK : (j + 1) * CHUNK, :])
        for copy in x_copies(k):
            copy.start()

    pack_rows(ORDER[: 2 * EARLY])
    pl.semaphore_wait(barrier, SHARDS - 1 + (GROUPS - 1) * CORES)
    for n in range(EARLY):
        send_rows(n)
    pack_rows(ORDER[2 * EARLY :])

    def both_cores(block):
        block = [
            jnp.maximum(block[k * CHUNK : (k + 1) * CHUNK, :], block[(k + 1) * CHUNK : (k + 2) * CHUNK, :])
            for k in range(0, CHUNKS, CORES)
        ]
        return jnp.concatenate(block, axis=0)

    def spread_lines(n, plane, held, sign):
        missing = jnp.zeros((LANES - PLANE, LANES), f32)
        turned = jnp.transpose(jnp.concatenate([plane, missing], axis=0))
        for m in range(LINES):
            tiles[n, m] = turned[m * CAP : (m + 1) * CAP, :]
        for m in range(1, LINES):
            pltpu.make_async_remote_copy(
                src_ref=tiles.at[n, m],
                dst_ref=held.at[m - 1],
                send_sem=tile_ss.at[n],
                recv_sem=tile_rs.at[n],
                device_id=along(sign * (m % GROUPS), m // GROUPS),
                device_id_type=MESH,
            ).start()

    def merge_lines(n, held):
        pltpu.make_async_copy(held, held, tile_rs.at[n]).wait()
        line = lax.broadcasted_iota(jnp.int32, (LANES, LANES), 0)
        merged = jnp.zeros((LANES, LANES), f32)
        for m in range(LINES):
            lines = held[m - 1] if m else tiles[n, 0]
            for r in range(CAP):
                merged = jnp.where(line == m * CAP + r, lines[r : r + 1, :], merged)
        return jnp.transpose(merged)[0:PLANE, :]

    others = pl.ds(1, PLANE - 1)

    def spread_rows(n, sent, held, sign):
        held[0] = sent[0]
        for row in range(1, PLANE):
            dy, dz, _ = steps(row // CHUNK * CORES * CHUNK + row % CHUNK)
            pltpu.make_async_remote_copy(
                src_ref=sent.at[row],
                dst_ref=held.at[row],
                send_sem=row_ss.at[n],
                recv_sem=row_rs.at[n],
                device_id=at(sign * dy, sign * dz, 0),
                device_id_type=MESH,
            ).start()

    def rows_arrived(n, held):
        pltpu.make_async_copy(held.at[others], held.at[others], row_rs.at[n]).wait()

    incoming[1].wait()
    cid = cid_ref[...].astype(f32) + 1.0
    lane = lax.broadcasted_iota(jnp.int32, (SHARDS, LANES), 1)
    core_lane = lax.broadcasted_iota(jnp.int32, (SHARDS, LANES), 0) // CHUNK % CORES * PAIR
    tags = jnp.zeros((SHARDS, LANES), f32)
    for j in range(PAIR):
        tag = jnp.sum(hot[j].astype(f32) * cid, axis=1, keepdims=True)
        tags = jnp.where(lane == core_lane + j, tag, tags)
    spread_lines(0, both_cores(tags) - 1.0, tag_xs, 1)

    total = SHARDS * PAIR
    lanes = lax.broadcasted_iota(jnp.int32, (total, LANES), 1)
    member = lax.broadcasted_iota(jnp.int32, (total, LANES), 0)
    mine = lanes == member // (CHUNK * PAIR) % CORES * PAIR + member % PAIR
    number = lax.broadcasted_iota(jnp.int32, (total, 1), 0)
    column = lax.broadcasted_iota(jnp.int32, (1, total), 1)

    def member_tags():
        rows_arrived(0, tag_recv)
        spread = jnp.broadcast_to(tag_recv[...], (PLANE, PAIR, LANES)).reshape(PLANE * PAIR, LANES)
        block = CHUNK * PAIR
        spread = [spread[k // CORES * block : (k // CORES + 1) * block, :] for k in range(CHUNKS)]
        spread = jnp.concatenate(spread, axis=0)
        tag_col = jnp.sum(jnp.where(mine, spread, 0.0), axis=1, keepdims=True)
        tag_col = jnp.where(tag_col < 0.0, -2.0 - number.astype(f32), tag_col)
        return tag_col, jnp.transpose(jnp.broadcast_to(tag_col, (total, LANES)))[0:1, :]

    def fold(scores):
        best = scores[:, 0:LANES]
        for first in range(LANES, scores.shape[1], LANES):
            best = jnp.maximum(best, scores[:, first : first + LANES])
        return best

    def score(begin, end):
        for k in range(begin // CHUNK, end // CHUNK):
            if k in ORDER[:EARLY]:
                recv[k * CHUNK : (k + 1) * CHUNK] = x_arrived(k)
            else:
                yz_arrived(k)
        low, high = begin * PAIR, end * PAIR
        scores = lax.dot_general(
            recv[0:end].reshape(high, features),
            recv[begin:end].reshape(high - low, features),
            (((1,), (1,)), ((), ())),
            preferred_element_type=f32,
        )
        scores = jnp.where(tag_col[0:high, :] == tag_row[:, low:high], scores, -1.0)
        own = scores[low:high, :]
        own = fold(jnp.where(number[low:high, :] != column[:, low:high], own, -1.0))
        if low:
            past = scores[0:low, :]
            peak[0:low, :] = jnp.maximum(peak[0:low, :], fold(past))
            past = jnp.max(past, axis=0, keepdims=True)
            past = jnp.transpose(jnp.broadcast_to(past, (LANES, high - low)))
            own = jnp.maximum(own, past)
        peak[low:high, :] = own

    steps_left = list(zip(SCORED[:-1], SCORED[1:]))
    for n in range(EARLY, CHUNKS):
        pass_rows(n)
        if n == TAGS_AFTER:
            tag_send[...] = merge_lines(0, tag_xs).reshape(PLANE, 1, LANES)
            spread_rows(0, tag_send, tag_recv, 1)
        if n in TURNS_AFTER:
            turn_rows(ORDER[TURNS_AFTER.index(n)])
        if n in SCORES_AFTER:
            if n == SCORES_AFTER[0]:
                tag_col, tag_row = member_tags()
            score(*steps_left.pop(0))
    for begin, end in steps_left:
        score(begin, end)
    best = jnp.max(peak[...], axis=1, keepdims=True)
    best = jnp.where(mine, best, -2.0)
    best = both_cores(jnp.max(best.reshape(SHARDS, PAIR, LANES), axis=1))
    ret_send[...] = best.reshape(PLANE, 1, LANES)

    spread_rows(1, ret_send, ret_recv, -1)
    rows_arrived(1, ret_recv)
    spread_lines(1, ret_recv[...].reshape(PLANE, LANES), ret_xs, -1)
    final = merge_lines(1, ret_xs)
    final = jnp.concatenate(
        [
            final[k // CORES * CHUNK : (k // CORES + 1) * CHUNK, k % CORES * PAIR : (k % CORES + 1) * PAIR]
            for k in range(CHUNKS)
        ],
        axis=0,
    )
    found = jnp.full((SHARDS, rows), -1.0, f32)
    for j in range(PAIR):
        found = jnp.maximum(found, jnp.where(hot[j] > 0.5, final[:, j : j + 1], -1.0))
    out_ref[...] = jnp.max(found, axis=0, keepdims=True)

    pltpu.make_async_copy(xsend, xsend, xs_sem).wait()
    part = ysend.at[pl.ds(1, SHARDS - 1)]
    pltpu.make_async_copy(part, part, ys_sem).wait()
    for n, held in enumerate((tag_xs, ret_xs)):
        pltpu.make_async_copy(held, held, tile_ss.at[n]).wait()
    for n, sent in enumerate((tag_send, ret_send)):
        pltpu.make_async_copy(sent.at[others], sent.at[others], row_ss.at[n]).wait()


def body(embeddings, cluster_id, row_targets):
    rows = embeddings.shape[0]
    features = embeddings.shape[1]
    copies = row_targets.shape[1]
    f32, bf16 = jnp.float32, jnp.bfloat16
    dma = pltpu.SemaphoreType.DMA

    held = pltpu.VMEM((LINES - 1, CAP, LANES), f32)
    small = pltpu.VMEM((PLANE, 1, LANES), f32)
    out = pl.pallas_call(
        kernel,
        out_shape=jax.ShapeDtypeStruct((1, rows), f32),
        in_specs=[pl.BlockSpec(memory_space=pltpu.HBM)] * 3,
        out_specs=pl.BlockSpec(memory_space=pltpu.VMEM),
        scratch_shapes=[
            pltpu.VMEM((rows, features), bf16),
            pltpu.VMEM((1, rows), jnp.int32),
            pltpu.VMEM((copies, rows), jnp.int32),
            pltpu.VMEM((rows, features), bf16),
            pltpu.VMEM((PAIR, SHARDS, rows), bf16),
            pltpu.VMEM((CHUNKS, GROUPS - 1, CAP * CHUNK, features), bf16),
            pltpu.VMEM((CHUNKS, GROUPS, CAP * CHUNK, features), bf16),
            pltpu.VMEM((SHARDS, PAIR, features), bf16),
            pltpu.VMEM((SHARDS, PAIR, features), bf16),
            pltpu.VMEM((SHARDS, PAIR, features), bf16),
            pltpu.VMEM((2, LINES, CAP, LANES), f32),
            held,
            held,
            small,
            small,
            small,
            small,
            pltpu.VMEM((SHARDS * PAIR, LANES), f32),
            dma((3,)),
            dma,
            dma((CHUNKS,)),
            dma,
            dma((CHUNKS,)),
            dma((2,)),
            dma((2,)),
            dma((2,)),
            dma((2,)),
        ],
        compiler_params=pltpu.CompilerParams(
            collective_id=0, has_side_effects=True, vmem_limit_bytes=63 * 2**20
        ),
        name="dedup",
    )(embeddings, cluster_id.reshape(1, rows), row_targets.T)
    return out.reshape(rows)


def solution(mesh):
    placed = (P(("shard", "grp"), None), P(("shard", "grp")), P(("shard", "grp"), None))
    return jax.shard_map(
        body, mesh=mesh, in_specs=placed, out_specs=P(("shard", "grp")), check_vma=False
    )
```

```python
import jax
import jax.numpy as jnp
from jax import lax
from jax.experimental import pallas as pl
from jax.experimental.pallas import tpu as pltpu
from jax.sharding import PartitionSpec as P

MESH = pl.DeviceIdType.MESH
SIDE = 8
CORES = 2
SHARDS = SIDE * SIDE * CORES
GROUPS = 4
CAP = 2
PAIR = GROUPS * CAP
LANES = 128
PLANE = SHARDS // CORES
LINES = GROUPS * CORES
CHUNK = 16
CHUNKS = SHARDS // CHUNK
ORDER = (4, 5, 0, 1, 2, 3, 6, 7)
EARLY = 2
TAGS_AFTER = 3
TURNS_AFTER = (4, 5)
SCORES_AFTER = (6, 7)
SCORED = (0, 32, 64, 96, 112, 128)


def sway(n):
    return (n + 1) // 2 * (n % 2 * 2 - 1) % SIDE


def steps(place):
    half = SIDE // 2
    chunk, pair, odd = place // CHUNK, place % CHUNK // 2, place % 2
    first = (chunk // CORES == 0) * 1
    sign = 1 - 2 * odd
    near, far = pair % half, pair // half
    dy = first * (sign * near + half * odd * ((near == 0) * 1)) + (1 - first) * sign * sway(pair)
    dz = dy + first * half * far + (1 - first) * sign * (chunk // CORES)
    return (dy + SIDE) % SIDE, (dz + 2 * SIDE) % SIDE, chunk % CORES


def shard_at(me, place, sign):
    dy, dz, dc = steps(place)
    y = (me // (SIDE * CORES) + sign * dy + SIDE) % SIDE
    z = ((me // CORES) % SIDE + sign * dz + SIDE) % SIDE
    c = (me + dc) % CORES
    return (y * SIDE + z) * CORES + c


def kernel(
    emb_hbm,
    cid_hbm,
    tgt_hbm,
    out_ref,
    emb_ref,
    cid_ref,
    tgt_ref,
    unit,
    hot,
    xsend,
    stage,
    ysend,
    recv,
    mid,
    tiles,
    tag_xs,
    ret_xs,
    tag_send,
    tag_recv,
    ret_send,
    ret_recv,
    peak,
    in_sem,
    xs_sem,
    xr_sem,
    ys_sem,
    yr_sem,
    tile_ss,
    tile_rs,
    row_ss,
    row_rs,
):
    rows, features = emb_ref.shape
    me = lax.axis_index("shard")
    grp = lax.axis_index("grp")
    f32 = jnp.float32
    bf16 = jnp.bfloat16

    incoming = [
        pltpu.make_async_copy(src, dst, in_sem.at[n])
        for n, (src, dst) in enumerate(
            [(tgt_hbm, tgt_ref), (cid_hbm, cid_ref), (emb_hbm, emb_ref)]
        )
    ]
    for copy in incoming:
        copy.start()

    ys = [(me // (SIDE * CORES) + d) % SIDE * (SIDE * CORES) for d in range(SIDE)]
    zs = [(me // CORES + d) % SIDE * CORES for d in range(SIDE)]
    cs = [(me + d) % CORES for d in range(CORES)]

    def at(dy, dz, dc):
        return {"shard": ys[dy % SIDE] + zs[dz % SIDE] + cs[dc]}

    def ahead(place):
        return at(*steps(place))

    def along(e, dc=0):
        return {"shard": ys[0] + zs[0] + cs[dc], "grp": (grp + e + GROUPS) % GROUPS}

    barrier = pltpu.get_barrier_semaphore()
    for e in range(1, GROUPS):
        for dc in range(CORES):
            pl.semaphore_signal(barrier, inc=1, device_id=along(e, dc), device_id_type=MESH)
    for place in range(1, SHARDS):
        pl.semaphore_signal(barrier, inc=1, device_id=ahead(place), device_id_type=MESH)

    place = lax.broadcasted_iota(jnp.int32, (SHARDS, 1), 0)
    peers = shard_at(me, place, 1) * GROUPS
    before = lax.broadcasted_iota(jnp.int32, (rows, rows), 0) < lax.broadcasted_iota(
        jnp.int32, (rows, rows), 1
    )
    before = jnp.where(before, 1.0, 0.0).astype(bf16)
    incoming[0].wait()
    named = []
    for e in range(GROUPS):
        target = peers + (grp + e) % GROUPS
        hit = tgt_ref[0:1, :] == target
        for c in range(1, tgt_ref.shape[0]):
            hit = hit | (tgt_ref[c : c + 1, :] == target)
        named.append(jnp.where(hit, 1.0, 0.0).astype(f32))
    named = jnp.concatenate(named, axis=0)
    rank = jnp.dot(named.astype(bf16), before, preferred_element_type=f32)
    for r in range(CAP):
        pick = jnp.where(rank == float(r), named, 0.0).astype(bf16)
        for e in range(GROUPS):
            hot[e * CAP + r] = pick[e * SHARDS : (e + 1) * SHARDS, :]

    incoming[2].wait()
    values = emb_ref[...].astype(f32)
    squares = jnp.sum(values * values, axis=1, keepdims=True)
    unit[...] = (values * lax.rsqrt(squares + 1e-06)).astype(bf16)

    size = PAIR * CHUNK
    order_out = lax.broadcasted_iota(jnp.int32, (size, size), 0)
    order_in = lax.broadcasted_iota(jnp.int32, (size, size), 1)
    turn = (order_in % CHUNK == order_out // PAIR) & (order_in // CHUNK == order_out % PAIR)
    turn = jnp.where(turn, 1.0, 0.0).astype(bf16)
    back = (order_out % CHUNK == order_in // PAIR) & (order_out // CHUNK == order_in % PAIR)
    back = jnp.where(back, 1.0, 0.0).astype(bf16)

    def by_place_first(block):
        block = jnp.dot(turn, block, preferred_element_type=f32).astype(bf16)
        return block.reshape(CHUNK, PAIR, features)

    def keep_for_x(k, j, block):
        e, r = j // CAP, j % CAP
        if e == 0:
            stage[k, 0, r * CHUNK : (r + 1) * CHUNK, :] = block
        else:
            xsend[k, e - 1, r * CHUNK : (r + 1) * CHUNK, :] = block

    def pack_rows(chunks):
        pick = [hot[j, k * CHUNK : (k + 1) * CHUNK, :] for k in chunks for j in range(PAIR)]
        packed = jnp.dot(
            jnp.concatenate(pick, axis=0), unit[...], preferred_element_type=f32
        ).astype(bf16)
        for n, k in enumerate(chunks):
            block = packed[n * size : (n + 1) * size, :]
            if k in ORDER[:EARLY]:
                ysend[k * CHUNK : (k + 1) * CHUNK] = by_place_first(block)
            else:
                for j in range(PAIR):
                    keep_for_x(k, j, block[j * CHUNK : (j + 1) * CHUNK, :])

    def x_copies(k):
        return [
            pltpu.make_async_remote_copy(
                src_ref=xsend.at[k, e - 1, pl.ds(r * CHUNK, CHUNK), columns],
                dst_ref=stage.at[k, e, pl.ds(r * CHUNK, CHUNK), columns],
                send_sem=xs_sem,
                recv_sem=xr_sem.at[k],
                device_id=along(e),
                device_id_type=MESH,
            )
            for r in range(CAP)
            for columns in (pl.ds(0, features // 2), pl.ds(features // 2, features // 2))
            for e in (1, 3, 2)
        ]

    def x_arrived(k):
        part = stage.at[k, pl.ds(1, GROUPS - 1)]
        pltpu.make_async_copy(part, part, xr_sem.at[k]).wait()
        return by_place_first(stage[k].reshape(size, features))

    def yz_arrived(k):
        first = max(1, k * CHUNK)
        part = pl.ds(first, (k + 1) * CHUNK - first)
        part = (mid if k in ORDER[:EARLY] else recv).at[part]
        pltpu.make_async_copy(part, part, yr_sem.at[k]).wait()

    def send_rows(n, later):
        k = ORDER[n]
        copies = [
            pltpu.make_async_remote_copy(
                src_ref=ysend.at[place],
                dst_ref=(mid if k in ORDER[:EARLY] else recv).at[place],
                send_sem=ys_sem,
                recv_sem=yr_sem.at[k],
                device_id=ahead(place),
                device_id_type=MESH,
            )
            for place in range(max(1, k * CHUNK), (k + 1) * CHUNK)
        ]
        between = [copy for m in later if m < CHUNKS for copy in x_copies(ORDER[m])]
        alone = len(copies)
        for m, copy in enumerate(between):
            copies.insert(m + (m + 1) * alone // (len(between) + 1), copy)
        for copy in copies:
            copy.start()

    def pass_rows(n):
        k = ORDER[n]
        ysend[k * CHUNK : (k + 1) * CHUNK] = x_arrived(k)
        if k == 0:
            recv[0] = ysend[0]
        send_rows(n, [n + EARLY])

    def turn_rows(k):
        yz_arrived(k)
        block = mid[k * CHUNK : (k + 1) * CHUNK].reshape(size, features)
        block = jnp.dot(back, block, preferred_element_type=f32).astype(bf16)
        for j in range(PAIR):
            keep_for_x(k, j, block[j * CHUNK : (j + 1) * CHUNK, :])
        for copy in x_copies(k):
            copy.start()

    pack_rows(ORDER[:1])
    pl.semaphore_wait(barrier, SHARDS - 1 + (GROUPS - 1) * CORES)
    send_rows(0, [])
    pack_rows(ORDER[1:4])
    send_rows(1, [2, 3])
    pack_rows(ORDER[4:])

    def both_cores(block):
        block = [
            jnp.maximum(block[k * CHUNK : (k + 1) * CHUNK, :], block[(k + 1) * CHUNK : (k + 2) * CHUNK, :])
            for k in range(0, CHUNKS, CORES)
        ]
        return jnp.concatenate(block, axis=0)

    def spread_lines(n, plane, held, sign):
        missing = jnp.zeros((LANES - PLANE, LANES), f32)
        turned = jnp.transpose(jnp.concatenate([plane, missing], axis=0))
        for m in range(LINES):
            tiles[n, m] = turned[m * CAP : (m + 1) * CAP, :]
        for m in range(1, LINES):
            pltpu.make_async_remote_copy(
                src_ref=tiles.at[n, m],
                dst_ref=held.at[m - 1],
                send_sem=tile_ss.at[n],
                recv_sem=tile_rs.at[n],
                device_id=along(sign * (m % GROUPS), m // GROUPS),
                device_id_type=MESH,
            ).start()

    def merge_lines(n, held):
        pltpu.make_async_copy(held, held, tile_rs.at[n]).wait()
        line = lax.broadcasted_iota(jnp.int32, (LANES, LANES), 0)
        merged = jnp.zeros((LANES, LANES), f32)
        for m in range(LINES):
            lines = held[m - 1] if m else tiles[n, 0]
            for r in range(CAP):
                merged = jnp.where(line == m * CAP + r, lines[r : r + 1, :], merged)
        return jnp.transpose(merged)[0:PLANE, :]

    others = pl.ds(1, PLANE - 1)

    def spread_rows(n, sent, held, sign):
        held[0] = sent[0]
        for row in range(1, PLANE):
            dy, dz, _ = steps(row // CHUNK * CORES * CHUNK + row % CHUNK)
            pltpu.make_async_remote_copy(
                src_ref=sent.at[row],
                dst_ref=held.at[row],
                send_sem=row_ss.at[n],
                recv_sem=row_rs.at[n],
                device_id=at(sign * dy, sign * dz, 0),
                device_id_type=MESH,
            ).start()

    def rows_arrived(n, held):
        pltpu.make_async_copy(held.at[others], held.at[others], row_rs.at[n]).wait()

    incoming[1].wait()
    cid = cid_ref[...].astype(f32) + 1.0
    lane = lax.broadcasted_iota(jnp.int32, (SHARDS, LANES), 1)
    core_lane = lax.broadcasted_iota(jnp.int32, (SHARDS, LANES), 0) // CHUNK % CORES * PAIR
    tags = jnp.zeros((SHARDS, LANES), f32)
    for j in range(PAIR):
        tag = jnp.sum(hot[j].astype(f32) * cid, axis=1, keepdims=True)
        tags = jnp.where(lane == core_lane + j, tag, tags)
    spread_lines(0, both_cores(tags) - 1.0, tag_xs, 1)

    total = SHARDS * PAIR
    lanes = lax.broadcasted_iota(jnp.int32, (total, LANES), 1)
    member = lax.broadcasted_iota(jnp.int32, (total, LANES), 0)
    mine = lanes == member // (CHUNK * PAIR) % CORES * PAIR + member % PAIR
    number = lax.broadcasted_iota(jnp.int32, (total, 1), 0)
    column = lax.broadcasted_iota(jnp.int32, (1, total), 1)

    def member_tags():
        rows_arrived(0, tag_recv)
        spread = jnp.broadcast_to(tag_recv[...], (PLANE, PAIR, LANES)).reshape(PLANE * PAIR, LANES)
        block = CHUNK * PAIR
        spread = [spread[k // CORES * block : (k // CORES + 1) * block, :] for k in range(CHUNKS)]
        spread = jnp.concatenate(spread, axis=0)
        tag_col = jnp.sum(jnp.where(mine, spread, 0.0), axis=1, keepdims=True)
        tag_col = jnp.where(tag_col < 0.0, -2.0 - number.astype(f32), tag_col)
        return tag_col, jnp.transpose(jnp.broadcast_to(tag_col, (total, LANES)))[0:1, :]

    def fold(scores):
        best = scores[:, 0:LANES]
        for first in range(LANES, scores.shape[1], LANES):
            best = jnp.maximum(best, scores[:, first : first + LANES])
        return best

    def score(begin, end):
        for k in range(begin // CHUNK, end // CHUNK):
            if k in ORDER[:EARLY]:
                recv[k * CHUNK : (k + 1) * CHUNK] = x_arrived(k)
            else:
                yz_arrived(k)
        low, high = begin * PAIR, end * PAIR
        scores = lax.dot_general(
            recv[0:end].reshape(high, features),
            recv[begin:end].reshape(high - low, features),
            (((1,), (1,)), ((), ())),
            preferred_element_type=f32,
        )
        scores = jnp.where(tag_col[0:high, :] == tag_row[:, low:high], scores, -1.0)
        own = scores[low:high, :]
        own = fold(jnp.where(number[low:high, :] != column[:, low:high], own, -1.0))
        if low:
            past = scores[0:low, :]
            peak[0:low, :] = jnp.maximum(peak[0:low, :], fold(past))
            past = jnp.max(past, axis=0, keepdims=True)
            past = jnp.transpose(jnp.broadcast_to(past, (LANES, high - low)))
            own = jnp.maximum(own, past)
        peak[low:high, :] = own

    steps_left = list(zip(SCORED[:-1], SCORED[1:]))
    for n in range(EARLY, CHUNKS):
        pass_rows(n)
        if n == TAGS_AFTER:
            tag_send[...] = merge_lines(0, tag_xs).reshape(PLANE, 1, LANES)
            spread_rows(0, tag_send, tag_recv, 1)
        if n in TURNS_AFTER:
            turn_rows(ORDER[TURNS_AFTER.index(n)])
        if n in SCORES_AFTER:
            if n == SCORES_AFTER[0]:
                tag_col, tag_row = member_tags()
            score(*steps_left.pop(0))
    for begin, end in steps_left:
        score(begin, end)
    best = jnp.max(peak[...], axis=1, keepdims=True)
    best = jnp.where(mine, best, -2.0)
    best = both_cores(jnp.max(best.reshape(SHARDS, PAIR, LANES), axis=1))
    ret_send[...] = best.reshape(PLANE, 1, LANES)

    spread_rows(1, ret_send, ret_recv, -1)
    rows_arrived(1, ret_recv)
    spread_lines(1, ret_recv[...].reshape(PLANE, LANES), ret_xs, -1)
    final = merge_lines(1, ret_xs)
    final = jnp.concatenate(
        [
            final[k // CORES * CHUNK : (k // CORES + 1) * CHUNK, k % CORES * PAIR : (k % CORES + 1) * PAIR]
            for k in range(CHUNKS)
        ],
        axis=0,
    )
    found = jnp.full((SHARDS, rows), -1.0, f32)
    for j in range(PAIR):
        found = jnp.maximum(found, jnp.where(hot[j] > 0.5, final[:, j : j + 1], -1.0))
    out_ref[...] = jnp.max(found, axis=0, keepdims=True)

    pltpu.make_async_copy(xsend, xsend, xs_sem).wait()
    part = ysend.at[pl.ds(1, SHARDS - 1)]
    pltpu.make_async_copy(part, part, ys_sem).wait()
    for n, held in enumerate((tag_xs, ret_xs)):
        pltpu.make_async_copy(held, held, tile_ss.at[n]).wait()
    for n, sent in enumerate((tag_send, ret_send)):
        pltpu.make_async_copy(sent.at[others], sent.at[others], row_ss.at[n]).wait()


def body(embeddings, cluster_id, row_targets):
    rows = embeddings.shape[0]
    features = embeddings.shape[1]
    copies = row_targets.shape[1]
    f32, bf16 = jnp.float32, jnp.bfloat16
    dma = pltpu.SemaphoreType.DMA

    held = pltpu.VMEM((LINES - 1, CAP, LANES), f32)
    small = pltpu.VMEM((PLANE, 1, LANES), f32)
    out = pl.pallas_call(
        kernel,
        out_shape=jax.ShapeDtypeStruct((1, rows), f32),
        in_specs=[pl.BlockSpec(memory_space=pltpu.HBM)] * 3,
        out_specs=pl.BlockSpec(memory_space=pltpu.VMEM),
        scratch_shapes=[
            pltpu.VMEM((rows, features), bf16),
            pltpu.VMEM((1, rows), jnp.int32),
            pltpu.VMEM((copies, rows), jnp.int32),
            pltpu.VMEM((rows, features), bf16),
            pltpu.VMEM((PAIR, SHARDS, rows), bf16),
            pltpu.VMEM((CHUNKS, GROUPS - 1, CAP * CHUNK, features), bf16),
            pltpu.VMEM((CHUNKS, GROUPS, CAP * CHUNK, features), bf16),
            pltpu.VMEM((SHARDS, PAIR, features), bf16),
            pltpu.VMEM((SHARDS, PAIR, features), bf16),
            pltpu.VMEM((SHARDS, PAIR, features), bf16),
            pltpu.VMEM((2, LINES, CAP, LANES), f32),
            held,
            held,
            small,
            small,
            small,
            small,
            pltpu.VMEM((SHARDS * PAIR, LANES), f32),
            dma((3,)),
            dma,
            dma((CHUNKS,)),
            dma,
            dma((CHUNKS,)),
            dma((2,)),
            dma((2,)),
            dma((2,)),
            dma((2,)),
        ],
        compiler_params=pltpu.CompilerParams(
            collective_id=0, has_side_effects=True, vmem_limit_bytes=63 * 2**20
        ),
        name="dedup",
    )(embeddings, cluster_id.reshape(1, rows), row_targets.T)
    return out.reshape(rows)


def solution(mesh):
    placed = (P(("shard", "grp"), None), P(("shard", "grp")), P(("shard", "grp"), None))
    return jax.shard_map(
        body, mesh=mesh, in_specs=placed, out_specs=P(("shard", "grp")), check_vma=False
    )
```

```python
import jax
import jax.numpy as jnp
from jax import lax
from jax.experimental import pallas as pl
from jax.experimental.pallas import tpu as pltpu
from jax.sharding import PartitionSpec as P

MESH = pl.DeviceIdType.MESH
SIDE = 8
CORES = 2
SHARDS = SIDE * SIDE * CORES
GROUPS = 4
CAP = 2
PAIR = GROUPS * CAP
LANES = 128
PLANE = SHARDS // CORES
LINES = GROUPS * CORES
CHUNK = 16
CHUNKS = SHARDS // CHUNK
ORDER = (2, 3, 4, 5, 0, 1, 6, 7)
EARLY = 4
TURNS = {4: [], 5: [0], 6: [1], 7: [2, 3]}
TAGS_AFTER = 5
SCORED = (0, 32, 64, 96, 112, 128)


def sway(n):
    return (n + 1) // 2 * (n % 2 * 2 - 1) % SIDE


def steps(place):
    half = SIDE // 2
    chunk, pair, odd = place // CHUNK, place % CHUNK // 2, place % 2
    first = (chunk // CORES == 0) * 1
    sign = 1 - 2 * odd
    near, far = pair % half, pair // half
    dy = first * (sign * near + half * odd * ((near == 0) * 1)) + (1 - first) * sign * sway(pair)
    dz = dy + first * half * far + (1 - first) * sign * (chunk // CORES)
    return (dy + SIDE) % SIDE, (dz + 2 * SIDE) % SIDE, chunk % CORES


def shard_at(me, place, sign):
    dy, dz, dc = steps(place)
    y = (me // (SIDE * CORES) + sign * dy + SIDE) % SIDE
    z = ((me // CORES) % SIDE + sign * dz + SIDE) % SIDE
    c = (me + dc) % CORES
    return (y * SIDE + z) * CORES + c


def kernel(
    emb_hbm,
    cid_hbm,
    tgt_hbm,
    out_ref,
    emb_ref,
    cid_ref,
    tgt_ref,
    unit,
    hot,
    xsend,
    stage,
    ysend,
    recv,
    mid,
    tiles,
    tag_xs,
    ret_xs,
    tag_send,
    tag_recv,
    ret_send,
    ret_recv,
    peak,
    in_sem,
    xs_sem,
    xr_sem,
    ys_sem,
    yr_sem,
    tile_ss,
    tile_rs,
    row_ss,
    row_rs,
):
    rows, features = emb_ref.shape
    me = lax.axis_index("shard")
    grp = lax.axis_index("grp")
    f32 = jnp.float32
    bf16 = jnp.bfloat16

    incoming = [
        pltpu.make_async_copy(src, dst, in_sem.at[n])
        for n, (src, dst) in enumerate(
            [(tgt_hbm, tgt_ref), (cid_hbm, cid_ref), (emb_hbm, emb_ref)]
        )
    ]
    for copy in incoming:
        copy.start()

    ys = [(me // (SIDE * CORES) + d) % SIDE * (SIDE * CORES) for d in range(SIDE)]
    zs = [(me // CORES + d) % SIDE * CORES for d in range(SIDE)]
    cs = [(me + d) % CORES for d in range(CORES)]

    def at(dy, dz, dc):
        return {"shard": ys[dy % SIDE] + zs[dz % SIDE] + cs[dc]}

    def ahead(place):
        return at(*steps(place))

    def along(e, dc=0):
        return {"shard": ys[0] + zs[0] + cs[dc], "grp": (grp + e + GROUPS) % GROUPS}

    barrier = pltpu.get_barrier_semaphore()
    for e in range(1, GROUPS):
        for dc in range(CORES):
            pl.semaphore_signal(barrier, inc=1, device_id=along(e, dc), device_id_type=MESH)
    for place in range(1, SHARDS):
        pl.semaphore_signal(barrier, inc=1, device_id=ahead(place), device_id_type=MESH)

    place = lax.broadcasted_iota(jnp.int32, (SHARDS, 1), 0)
    peers = shard_at(me, place, 1) * GROUPS
    before = lax.broadcasted_iota(jnp.int32, (rows, rows), 0) < lax.broadcasted_iota(
        jnp.int32, (rows, rows), 1
    )
    before = jnp.where(before, 1.0, 0.0).astype(bf16)
    incoming[0].wait()
    named = []
    for e in range(GROUPS):
        target = peers + (grp + e) % GROUPS
        hit = tgt_ref[0:1, :] == target
        for c in range(1, tgt_ref.shape[0]):
            hit = hit | (tgt_ref[c : c + 1, :] == target)
        named.append(jnp.where(hit, 1.0, 0.0).astype(f32))
    named = jnp.concatenate(named, axis=0)
    rank = jnp.dot(named.astype(bf16), before, preferred_element_type=f32)
    for r in range(CAP):
        pick = jnp.where(rank == float(r), named, 0.0).astype(bf16)
        for e in range(GROUPS):
            hot[e * CAP + r] = pick[e * SHARDS : (e + 1) * SHARDS, :]

    incoming[2].wait()
    values = emb_ref[...].astype(f32)
    squares = jnp.sum(values * values, axis=1, keepdims=True)
    unit[...] = (values * lax.rsqrt(squares + 1e-06)).astype(bf16)

    size = PAIR * CHUNK
    order_out = lax.broadcasted_iota(jnp.int32, (size, size), 0)
    order_in = lax.broadcasted_iota(jnp.int32, (size, size), 1)
    turn = (order_in % CHUNK == order_out // PAIR) & (order_in // CHUNK == order_out % PAIR)
    turn = jnp.where(turn, 1.0, 0.0).astype(bf16)
    back = (order_out % CHUNK == order_in // PAIR) & (order_out // CHUNK == order_in % PAIR)
    back = jnp.where(back, 1.0, 0.0).astype(bf16)

    def by_place_first(block):
        block = jnp.dot(turn, block, preferred_element_type=f32).astype(bf16)
        return block.reshape(CHUNK, PAIR, features)

    def keep_for_x(k, j, block):
        e, r = j // CAP, j % CAP
        if e == 0:
            stage[k, 0, r * CHUNK : (r + 1) * CHUNK, :] = block
        else:
            xsend[k, e - 1, r * CHUNK : (r + 1) * CHUNK, :] = block

    def pack_rows(chunks):
        pick = [hot[j, k * CHUNK : (k + 1) * CHUNK, :] for k in chunks for j in range(PAIR)]
        packed = jnp.dot(
            jnp.concatenate(pick, axis=0), unit[...], preferred_element_type=f32
        ).astype(bf16)
        for n, k in enumerate(chunks):
            block = packed[n * size : (n + 1) * size, :]
            if k in ORDER[:EARLY]:
                ysend[k * CHUNK : (k + 1) * CHUNK] = by_place_first(block)
            else:
                for j in range(PAIR):
                    keep_for_x(k, j, block[j * CHUNK : (j + 1) * CHUNK, :])

    def x_copies(k):
        return [
            pltpu.make_async_remote_copy(
                src_ref=xsend.at[k, e - 1, pl.ds(r * CHUNK, CHUNK)],
                dst_ref=stage.at[k, e, pl.ds(r * CHUNK, CHUNK)],
                send_sem=xs_sem,
                recv_sem=xr_sem.at[k],
                device_id=along(e),
                device_id_type=MESH,
            )
            for r in range(CAP)
            for e in (1, 3, 2)
        ]

    def x_arrived(k):
        part = stage.at[k, pl.ds(1, GROUPS - 1)]
        pltpu.make_async_copy(part, part, xr_sem.at[k]).wait()
        return by_place_first(stage[k].reshape(size, features))

    def yz_arrived(k):
        first = max(1, k * CHUNK)
        part = pl.ds(first, (k + 1) * CHUNK - first)
        part = (mid if k in ORDER[:EARLY] else recv).at[part]
        pltpu.make_async_copy(part, part, yr_sem.at[k]).wait()

    def send_rows(n, later):
        k = ORDER[n]
        copies = [
            pltpu.make_async_remote_copy(
                src_ref=ysend.at[place],
                dst_ref=(mid if k in ORDER[:EARLY] else recv).at[place],
                send_sem=ys_sem,
                recv_sem=yr_sem.at[k],
                device_id=ahead(place),
                device_id_type=MESH,
            )
            for place in range(max(1, k * CHUNK), (k + 1) * CHUNK)
        ]
        between = [copy for m in later for copy in x_copies(ORDER[m])]
        alone = len(copies)
        for m, copy in enumerate(between):
            copies.insert(m + (m + 1) * alone // (len(between) + 1), copy)
        for copy in copies:
            copy.start()

    def pass_rows(n, later):
        k = ORDER[n]
        ysend[k * CHUNK : (k + 1) * CHUNK] = x_arrived(k)
        if k == 0:
            recv[0] = ysend[0]
        send_rows(n, later)

    def turn_rows(k):
        yz_arrived(k)
        block = mid[k * CHUNK : (k + 1) * CHUNK].reshape(size, features)
        block = jnp.dot(back, block, preferred_element_type=f32).astype(bf16)
        for j in range(PAIR):
            keep_for_x(k, j, block[j * CHUNK : (j + 1) * CHUNK, :])

    for n in range(EARLY):
        pack_rows([ORDER[n], ORDER[n + EARLY]])
        if n == 0:
            pl.semaphore_wait(barrier, SHARDS - 1 + (GROUPS - 1) * CORES)
        send_rows(n, [n + EARLY])

    def both_cores(block):
        block = [
            jnp.maximum(block[k * CHUNK : (k + 1) * CHUNK, :], block[(k + 1) * CHUNK : (k + 2) * CHUNK, :])
            for k in range(0, CHUNKS, CORES)
        ]
        return jnp.concatenate(block, axis=0)

    def spread_lines(n, plane, held, sign):
        missing = jnp.zeros((LANES - PLANE, LANES), f32)
        turned = jnp.transpose(jnp.concatenate([plane, missing], axis=0))
        for m in range(LINES):
            tiles[n, m] = turned[m * CAP : (m + 1) * CAP, :]
        for m in range(1, LINES):
            pltpu.make_async_remote_copy(
                src_ref=tiles.at[n, m],
                dst_ref=held.at[m - 1],
                send_sem=tile_ss.at[n],
                recv_sem=tile_rs.at[n],
                device_id=along(sign * (m % GROUPS), m // GROUPS),
                device_id_type=MESH,
            ).start()

    def merge_lines(n, held):
        pltpu.make_async_copy(held, held, tile_rs.at[n]).wait()
        line = lax.broadcasted_iota(jnp.int32, (LANES, LANES), 0)
        merged = jnp.zeros((LANES, LANES), f32)
        for m in range(LINES):
            lines = held[m - 1] if m else tiles[n, 0]
            for r in range(CAP):
                merged = jnp.where(line == m * CAP + r, lines[r : r + 1, :], merged)
        return jnp.transpose(merged)[0:PLANE, :]

    others = pl.ds(1, PLANE - 1)

    def spread_rows(n, sent, held, sign):
        held[0] = sent[0]
        for row in range(1, PLANE):
            dy, dz, _ = steps(row // CHUNK * CORES * CHUNK + row % CHUNK)
            pltpu.make_async_remote_copy(
                src_ref=sent.at[row],
                dst_ref=held.at[row],
                send_sem=row_ss.at[n],
                recv_sem=row_rs.at[n],
                device_id=at(sign * dy, sign * dz, 0),
                device_id_type=MESH,
            ).start()

    def rows_arrived(n, held):
        pltpu.make_async_copy(held.at[others], held.at[others], row_rs.at[n]).wait()

    incoming[1].wait()
    cid = cid_ref[...].astype(f32) + 1.0
    lane = lax.broadcasted_iota(jnp.int32, (SHARDS, LANES), 1)
    core_lane = lax.broadcasted_iota(jnp.int32, (SHARDS, LANES), 0) // CHUNK % CORES * PAIR
    tags = jnp.zeros((SHARDS, LANES), f32)
    for j in range(PAIR):
        tag = jnp.sum(hot[j].astype(f32) * cid, axis=1, keepdims=True)
        tags = jnp.where(lane == core_lane + j, tag, tags)
    spread_lines(0, both_cores(tags) - 1.0, tag_xs, 1)

    total = SHARDS * PAIR
    lanes = lax.broadcasted_iota(jnp.int32, (total, LANES), 1)
    member = lax.broadcasted_iota(jnp.int32, (total, LANES), 0)
    mine = lanes == member // (CHUNK * PAIR) % CORES * PAIR + member % PAIR
    number = lax.broadcasted_iota(jnp.int32, (total, 1), 0)
    column = lax.broadcasted_iota(jnp.int32, (1, total), 1)

    def member_tags():
        rows_arrived(0, tag_recv)
        spread = jnp.broadcast_to(tag_recv[...], (PLANE, PAIR, LANES)).reshape(PLANE * PAIR, LANES)
        block = CHUNK * PAIR
        spread = [spread[k // CORES * block : (k // CORES + 1) * block, :] for k in range(CHUNKS)]
        spread = jnp.concatenate(spread, axis=0)
        tag_col = jnp.sum(jnp.where(mine, spread, 0.0), axis=1, keepdims=True)
        tag_col = jnp.where(tag_col < 0.0, -2.0 - number.astype(f32), tag_col)
        return tag_col, jnp.transpose(jnp.broadcast_to(tag_col, (total, LANES)))[0:1, :]

    def fold(scores):
        best = scores[:, 0:LANES]
        for first in range(LANES, scores.shape[1], LANES):
            best = jnp.maximum(best, scores[:, first : first + LANES])
        return best

    def score(begin, end):
        for k in range(begin // CHUNK, end // CHUNK):
            if k in ORDER[:EARLY]:
                recv[k * CHUNK : (k + 1) * CHUNK] = x_arrived(k)
            else:
                yz_arrived(k)
        low, high = begin * PAIR, end * PAIR
        scores = lax.dot_general(
            recv[0:end].reshape(high, features),
            recv[begin:end].reshape(high - low, features),
            (((1,), (1,)), ((), ())),
            preferred_element_type=f32,
        )
        scores = jnp.where(tag_col[0:high, :] == tag_row[:, low:high], scores, -1.0)
        own = scores[low:high, :]
        own = fold(jnp.where(number[low:high, :] != column[:, low:high], own, -1.0))
        if low:
            past = scores[0:low, :]
            peak[0:low, :] = jnp.maximum(peak[0:low, :], fold(past))
            past = jnp.max(past, axis=0, keepdims=True)
            past = jnp.transpose(jnp.broadcast_to(past, (LANES, high - low)))
            own = jnp.maximum(own, past)
        peak[low:high, :] = own

    for n in range(EARLY, CHUNKS):
        for m in TURNS[n]:
            turn_rows(ORDER[m])
        pass_rows(n, TURNS[n])
        if n == TAGS_AFTER:
            tag_send[...] = merge_lines(0, tag_xs).reshape(PLANE, 1, LANES)
            spread_rows(0, tag_send, tag_recv, 1)
    tag_col, tag_row = member_tags()
    for begin, end in zip(SCORED[:-1], SCORED[1:]):
        score(begin, end)
    best = jnp.max(peak[...], axis=1, keepdims=True)
    best = jnp.where(mine, best, -2.0)
    best = both_cores(jnp.max(best.reshape(SHARDS, PAIR, LANES), axis=1))
    ret_send[...] = best.reshape(PLANE, 1, LANES)

    spread_rows(1, ret_send, ret_recv, -1)
    rows_arrived(1, ret_recv)
    spread_lines(1, ret_recv[...].reshape(PLANE, LANES), ret_xs, -1)
    final = merge_lines(1, ret_xs)
    final = jnp.concatenate(
        [
            final[k // CORES * CHUNK : (k // CORES + 1) * CHUNK, k % CORES * PAIR : (k % CORES + 1) * PAIR]
            for k in range(CHUNKS)
        ],
        axis=0,
    )
    found = jnp.full((SHARDS, rows), -1.0, f32)
    for j in range(PAIR):
        found = jnp.maximum(found, jnp.where(hot[j] > 0.5, final[:, j : j + 1], -1.0))
    out_ref[...] = jnp.max(found, axis=0, keepdims=True)

    pltpu.make_async_copy(xsend, xsend, xs_sem).wait()
    part = ysend.at[pl.ds(1, SHARDS - 1)]
    pltpu.make_async_copy(part, part, ys_sem).wait()
    for n, held in enumerate((tag_xs, ret_xs)):
        pltpu.make_async_copy(held, held, tile_ss.at[n]).wait()
    for n, sent in enumerate((tag_send, ret_send)):
        pltpu.make_async_copy(sent.at[others], sent.at[others], row_ss.at[n]).wait()


def body(embeddings, cluster_id, row_targets):
    rows = embeddings.shape[0]
    features = embeddings.shape[1]
    copies = row_targets.shape[1]
    f32, bf16 = jnp.float32, jnp.bfloat16
    dma = pltpu.SemaphoreType.DMA

    held = pltpu.VMEM((LINES - 1, CAP, LANES), f32)
    small = pltpu.VMEM((PLANE, 1, LANES), f32)
    out = pl.pallas_call(
        kernel,
        out_shape=jax.ShapeDtypeStruct((1, rows), f32),
        in_specs=[pl.BlockSpec(memory_space=pltpu.HBM)] * 3,
        out_specs=pl.BlockSpec(memory_space=pltpu.VMEM),
        scratch_shapes=[
            pltpu.VMEM((rows, features), bf16),
            pltpu.VMEM((1, rows), jnp.int32),
            pltpu.VMEM((copies, rows), jnp.int32),
            pltpu.VMEM((rows, features), bf16),
            pltpu.VMEM((PAIR, SHARDS, rows), bf16),
            pltpu.VMEM((CHUNKS, GROUPS - 1, CAP * CHUNK, features), bf16),
            pltpu.VMEM((CHUNKS, GROUPS, CAP * CHUNK, features), bf16),
            pltpu.VMEM((SHARDS, PAIR, features), bf16),
            pltpu.VMEM((SHARDS, PAIR, features), bf16),
            pltpu.VMEM((SHARDS, PAIR, features), bf16),
            pltpu.VMEM((2, LINES, CAP, LANES), f32),
            held,
            held,
            small,
            small,
            small,
            small,
            pltpu.VMEM((SHARDS * PAIR, LANES), f32),
            dma((3,)),
            dma,
            dma((CHUNKS,)),
            dma,
            dma((CHUNKS,)),
            dma((2,)),
            dma((2,)),
            dma((2,)),
            dma((2,)),
        ],
        compiler_params=pltpu.CompilerParams(
            collective_id=0, has_side_effects=True, vmem_limit_bytes=63 * 2**20
        ),
        name="dedup",
    )(embeddings, cluster_id.reshape(1, rows), row_targets.T)
    return out.reshape(rows)


def solution(mesh):
    placed = (P(("shard", "grp"), None), P(("shard", "grp")), P(("shard", "grp"), None))
    return jax.shard_map(
        body, mesh=mesh, in_specs=placed, out_specs=P(("shard", "grp")), check_vma=False
    )
```

```python
import jax
import jax.numpy as jnp
from jax import lax
from jax.experimental import pallas as pl
from jax.experimental.pallas import tpu as pltpu
from jax.sharding import PartitionSpec as P

MESH = pl.DeviceIdType.MESH
SIDE = 8
CORES = 2
SHARDS = SIDE * SIDE * CORES
GROUPS = 4
CAP = 2
PAIR = GROUPS * CAP
LANES = 128
CHUNK = 16
CHUNKS = SHARDS // CHUNK
ORDER = (4, 5, 0, 1, 2, 3, 6, 7)
EARLY = 2
TAGS_AFTER = 3
TURNS_AFTER = (4, 5)
SCORES_AFTER = (6, 7)
SCORED = (0, 32, 64, 96, 112, 128)


def sway(n):
    return (n + 1) // 2 * (n % 2 * 2 - 1) % SIDE


def steps(place):
    half = SIDE // 2
    chunk, pair, odd = place // CHUNK, place % CHUNK // 2, place % 2
    first = (chunk // CORES == 0) * 1
    sign = 1 - 2 * odd
    near, far = pair % half, pair // half
    dy = first * (sign * near + half * odd * ((near == 0) * 1)) + (1 - first) * sign * sway(pair)
    dz = dy + first * half * far + (1 - first) * sign * (chunk // CORES)
    return (dy + SIDE) % SIDE, (dz + 2 * SIDE) % SIDE, chunk % CORES


def shard_at(me, place, way):
    dy, dz, dc = steps(place)
    y = (me // (SIDE * CORES) + way * dy + SIDE) % SIDE
    z = ((me // CORES) % SIDE + way * dz + SIDE) % SIDE
    c = (me + dc) % CORES
    return (y * SIDE + z) * CORES + c


def kernel(
    emb_hbm,
    cid_hbm,
    tgt_hbm,
    out_ref,
    emb_ref,
    cid_ref,
    tgt_ref,
    unit,
    hot,
    xsend,
    stage,
    ysend,
    recv,
    mid,
    tiles,
    tag_xs,
    ret_xs,
    tag_send,
    tag_recv,
    ret_send,
    ret_recv,
    peak,
    in_sem,
    xs_sem,
    xr_sem,
    ys_sem,
    yr_sem,
    tile_ss,
    tile_rs,
    row_ss,
    row_rs,
):
    rows, features = emb_ref.shape
    me = lax.axis_index("shard")
    grp = lax.axis_index("grp")
    f32 = jnp.float32
    bf16 = jnp.bfloat16

    incoming = [
        pltpu.make_async_copy(src, dst, in_sem.at[n])
        for n, (src, dst) in enumerate(
            [(tgt_hbm, tgt_ref), (cid_hbm, cid_ref), (emb_hbm, emb_ref)]
        )
    ]
    for copy in incoming:
        copy.start()

    way = 1 - me % CORES * 2
    ys = [(me // (SIDE * CORES) + way * d + SIDE) % SIDE * (SIDE * CORES) for d in range(SIDE)]
    zs = [(me // CORES + way * d + SIDE) % SIDE * CORES for d in range(SIDE)]
    cs = [(me + d) % CORES for d in range(CORES)]

    def at(dy, dz, dc):
        return {"shard": ys[dy % SIDE] + zs[dz % SIDE] + cs[dc]}

    def ahead(place):
        return at(*steps(place))

    def behind(place):
        dy, dz, dc = steps(place)
        return at(dy, dz, dc) if dc else at(-dy, -dz, dc)

    def along(e):
        return {"grp": (grp + e + GROUPS) % GROUPS}

    barrier = pltpu.get_barrier_semaphore()
    for e in range(1, GROUPS):
        pl.semaphore_signal(
            barrier, inc=1, device_id=along(e), device_id_type=MESH
        )
    for place in range(1, SHARDS):
        pl.semaphore_signal(barrier, inc=1, device_id=ahead(place), device_id_type=MESH)

    place = lax.broadcasted_iota(jnp.int32, (SHARDS, 1), 0)
    peers = shard_at(me, place, way) * GROUPS
    before = lax.broadcasted_iota(jnp.int32, (rows, rows), 0) < lax.broadcasted_iota(
        jnp.int32, (rows, rows), 1
    )
    before = jnp.where(before, 1.0, 0.0).astype(bf16)
    incoming[0].wait()
    named = []
    for e in range(GROUPS):
        target = peers + (grp + e) % GROUPS
        hit = tgt_ref[0:1, :] == target
        for c in range(1, tgt_ref.shape[0]):
            hit = hit | (tgt_ref[c : c + 1, :] == target)
        named.append(jnp.where(hit, 1.0, 0.0).astype(f32))
    named = jnp.concatenate(named, axis=0)
    rank = jnp.dot(named.astype(bf16), before, preferred_element_type=f32)
    for r in range(CAP):
        pick = jnp.where(rank == float(r), named, 0.0).astype(bf16)
        for e in range(GROUPS):
            hot[e * CAP + r] = pick[e * SHARDS : (e + 1) * SHARDS, :]

    incoming[2].wait()
    values = emb_ref[...].astype(f32)
    squares = jnp.sum(values * values, axis=1, keepdims=True)
    unit[...] = (values * lax.rsqrt(squares + 1e-06)).astype(bf16)

    size = PAIR * CHUNK
    order_out = lax.broadcasted_iota(jnp.int32, (size, size), 0)
    order_in = lax.broadcasted_iota(jnp.int32, (size, size), 1)
    turn = (order_in % CHUNK == order_out // PAIR) & (order_in // CHUNK == order_out % PAIR)
    turn = jnp.where(turn, 1.0, 0.0).astype(bf16)
    back = (order_out % CHUNK == order_in // PAIR) & (order_out // CHUNK == order_in % PAIR)
    back = jnp.where(back, 1.0, 0.0).astype(bf16)

    def by_place_first(block):
        block = jnp.dot(turn, block, preferred_element_type=f32).astype(bf16)
        return block.reshape(CHUNK, PAIR, features)

    def keep_for_x(k, j, block):
        e, r = j // CAP, j % CAP
        if e == 0:
            stage[k, 0, r * CHUNK : (r + 1) * CHUNK, :] = block
        else:
            xsend[k, e - 1, r * CHUNK : (r + 1) * CHUNK, :] = block

    def pack_rows(chunks):
        pick = [hot[j, k * CHUNK : (k + 1) * CHUNK, :] for k in chunks for j in range(PAIR)]
        packed = jnp.dot(
            jnp.concatenate(pick, axis=0), unit[...], preferred_element_type=f32
        ).astype(bf16)
        for n, k in enumerate(chunks):
            block = packed[n * size : (n + 1) * size, :]
            if k in ORDER[:EARLY]:
                ysend[k * CHUNK : (k + 1) * CHUNK] = by_place_first(block)
            else:
                for j in range(PAIR):
                    keep_for_x(k, j, block[j * CHUNK : (j + 1) * CHUNK, :])

    def x_copies(k):
        return [
            pltpu.make_async_remote_copy(
                src_ref=xsend.at[k, e - 1, pl.ds(r * CHUNK, CHUNK)],
                dst_ref=stage.at[k, e, pl.ds(r * CHUNK, CHUNK)],
                send_sem=xs_sem,
                recv_sem=xr_sem.at[k],
                device_id=along(e),
                device_id_type=MESH,
            )
            for r in range(CAP)
            for e in (1, 3, 2)
        ]

    def x_arrived(k):
        part = stage.at[k, pl.ds(1, GROUPS - 1)]
        pltpu.make_async_copy(part, part, xr_sem.at[k]).wait()
        return by_place_first(stage[k].reshape(size, features))

    def yz_arrived(k):
        first = max(1, k * CHUNK)
        part = pl.ds(first, (k + 1) * CHUNK - first)
        part = (mid if k in ORDER[:EARLY] else recv).at[part]
        pltpu.make_async_copy(part, part, yr_sem.at[k]).wait()

    def send_rows(n):
        k = ORDER[n]
        copies = [
            pltpu.make_async_remote_copy(
                src_ref=ysend.at[place],
                dst_ref=(mid if k in ORDER[:EARLY] else recv).at[place],
                send_sem=ys_sem,
                recv_sem=yr_sem.at[k],
                device_id=ahead(place),
                device_id_type=MESH,
            )
            for place in range(max(1, k * CHUNK), (k + 1) * CHUNK)
        ]
        if n + EARLY < CHUNKS:
            between = x_copies(ORDER[n + EARLY])
            for m, copy in enumerate(between):
                copies.insert(m + (m + 1) * CHUNK // (len(between) + 1), copy)
        for copy in copies:
            copy.start()

    def pass_rows(n):
        k = ORDER[n]
        ysend[k * CHUNK : (k + 1) * CHUNK] = x_arrived(k)
        if k == 0:
            recv[0] = ysend[0]
        send_rows(n)

    def turn_rows(k):
        yz_arrived(k)
        block = mid[k * CHUNK : (k + 1) * CHUNK].reshape(size, features)
        block = jnp.dot(back, block, preferred_element_type=f32).astype(bf16)
        for j in range(PAIR):
            keep_for_x(k, j, block[j * CHUNK : (j + 1) * CHUNK, :])
        for copy in x_copies(k):
            copy.start()

    pack_rows(ORDER[: 2 * EARLY])
    pl.semaphore_wait(barrier, SHARDS - 1 + GROUPS - 1)
    for n in range(EARLY):
        send_rows(n)
    pack_rows(ORDER[2 * EARLY :])

    row8 = lax.broadcasted_iota(jnp.int32, (PAIR, LANES), 0) // CAP

    def spread_tile(n, held, sign):
        for e in range(1, GROUPS):
            pltpu.make_async_remote_copy(
                src_ref=tiles.at[n],
                dst_ref=held.at[e - 1],
                send_sem=tile_ss.at[n],
                recv_sem=tile_rs.at[n],
                device_id=along(sign * e),
                device_id_type=MESH,
            ).start()

    def merge_tile(n, held):
        pltpu.make_async_copy(held, held, tile_rs.at[n]).wait()
        merged = tiles[n]
        for e in range(1, GROUPS):
            merged = jnp.where(row8 == e, held[e - 1], merged)
        return jnp.transpose(
            jnp.concatenate([merged, jnp.zeros((LANES - PAIR, LANES), f32)], axis=0)
        )

    others = pl.ds(1, SHARDS - 1)

    def spread_rows(n, sent, held, device):
        held[0] = sent[0]
        for place in range(1, SHARDS):
            pltpu.make_async_remote_copy(
                src_ref=sent.at[place],
                dst_ref=held.at[place],
                send_sem=row_ss.at[n],
                recv_sem=row_rs.at[n],
                device_id=device(place),
                device_id_type=MESH,
            ).start()

    def rows_arrived(n, held):
        pltpu.make_async_copy(held.at[others], held.at[others], row_rs.at[n]).wait()

    incoming[1].wait()
    cid = cid_ref[...].astype(f32) + 1.0
    lane = lax.broadcasted_iota(jnp.int32, (SHARDS, LANES), 1)
    tags = jnp.zeros((SHARDS, LANES), f32)
    for j in range(PAIR):
        tag = jnp.sum(hot[j].astype(f32) * cid, axis=1, keepdims=True)
        tags = jnp.where(lane == j, tag, tags)
    tiles[0] = jnp.transpose(tags)[0:PAIR, :] - 1.0
    spread_tile(0, tag_xs, 1)

    total = SHARDS * PAIR
    lanes = lax.broadcasted_iota(jnp.int32, (total, LANES), 1)
    member = lax.broadcasted_iota(jnp.int32, (total, LANES), 0)
    mine = lanes == member % PAIR
    number = lax.broadcasted_iota(jnp.int32, (total, 1), 0)
    column = lax.broadcasted_iota(jnp.int32, (1, total), 1)

    def member_tags():
        rows_arrived(0, tag_recv)
        spread = jnp.broadcast_to(tag_recv[...], (SHARDS, PAIR, LANES)).reshape(total, LANES)
        tag_col = jnp.sum(jnp.where(mine, spread, 0.0), axis=1, keepdims=True)
        tag_col = jnp.where(tag_col < 0.0, -2.0 - number.astype(f32), tag_col)
        return tag_col, jnp.transpose(jnp.broadcast_to(tag_col, (total, LANES)))[0:1, :]

    def fold(scores):
        best = scores[:, 0:LANES]
        for first in range(LANES, scores.shape[1], LANES):
            best = jnp.maximum(best, scores[:, first : first + LANES])
        return best

    def score(begin, end):
        for k in range(begin // CHUNK, end // CHUNK):
            if k in ORDER[:EARLY]:
                recv[k * CHUNK : (k + 1) * CHUNK] = x_arrived(k)
            else:
                yz_arrived(k)
        low, high = begin * PAIR, end * PAIR
        scores = lax.dot_general(
            recv[0:end].reshape(high, features),
            recv[begin:end].reshape(high - low, features),
            (((1,), (1,)), ((), ())),
            preferred_element_type=f32,
        )
        scores = jnp.where(tag_col[0:high, :] == tag_row[:, low:high], scores, -1.0)
        own = scores[low:high, :]
        own = fold(jnp.where(number[low:high, :] != column[:, low:high], own, -1.0))
        if low:
            past = scores[0:low, :]
            peak[0:low, :] = jnp.maximum(peak[0:low, :], fold(past))
            past = jnp.max(past, axis=0, keepdims=True)
            past = jnp.transpose(jnp.broadcast_to(past, (LANES, high - low)))
            own = jnp.maximum(own, past)
        peak[low:high, :] = own

    steps_left = list(zip(SCORED[:-1], SCORED[1:]))
    for n in range(EARLY, CHUNKS):
        pass_rows(n)
        if n == TAGS_AFTER:
            tag_send[...] = merge_tile(0, tag_xs).reshape(SHARDS, 1, LANES)
            spread_rows(0, tag_send, tag_recv, ahead)
        if n in TURNS_AFTER:
            turn_rows(ORDER[TURNS_AFTER.index(n)])
        if n in SCORES_AFTER:
            if n == SCORES_AFTER[0]:
                tag_col, tag_row = member_tags()
            score(*steps_left.pop(0))
    for begin, end in steps_left:
        score(begin, end)
    best = jnp.max(peak[...], axis=1, keepdims=True)
    best = jnp.where(mine, best, -2.0)
    ret_send[...] = jnp.max(best.reshape(SHARDS, PAIR, LANES), axis=1, keepdims=True)

    spread_rows(1, ret_send, ret_recv, behind)
    rows_arrived(1, ret_recv)
    tiles[1] = jnp.transpose(ret_recv[...].reshape(SHARDS, LANES))[0:PAIR, :]
    spread_tile(1, ret_xs, -1)
    final = merge_tile(1, ret_xs)
    found = jnp.full((SHARDS, rows), -1.0, f32)
    for j in range(PAIR):
        found = jnp.maximum(found, jnp.where(hot[j] > 0.5, final[:, j : j + 1], -1.0))
    out_ref[...] = jnp.max(found, axis=0, keepdims=True)

    pltpu.make_async_copy(xsend, xsend, xs_sem).wait()
    pltpu.make_async_copy(ysend.at[others], ysend.at[others], ys_sem).wait()
    for n, held in enumerate((tag_xs, ret_xs)):
        pltpu.make_async_copy(held, held, tile_ss.at[n]).wait()
    for n, sent in enumerate((tag_send, ret_send)):
        pltpu.make_async_copy(sent.at[others], sent.at[others], row_ss.at[n]).wait()


def body(embeddings, cluster_id, row_targets):
    rows = embeddings.shape[0]
    features = embeddings.shape[1]
    copies = row_targets.shape[1]
    f32, bf16 = jnp.float32, jnp.bfloat16
    dma = pltpu.SemaphoreType.DMA

    def held(count):
        return pltpu.VMEM((count, PAIR, LANES), f32)

    small = pltpu.VMEM((SHARDS, 1, LANES), f32)

    out = pl.pallas_call(
        kernel,
        out_shape=jax.ShapeDtypeStruct((1, rows), f32),
        in_specs=[pl.BlockSpec(memory_space=pltpu.HBM)] * 3,
        out_specs=pl.BlockSpec(memory_space=pltpu.VMEM),
        scratch_shapes=[
            pltpu.VMEM((rows, features), bf16),
            pltpu.VMEM((1, rows), jnp.int32),
            pltpu.VMEM((copies, rows), jnp.int32),
            pltpu.VMEM((rows, features), bf16),
            pltpu.VMEM((PAIR, SHARDS, rows), bf16),
            pltpu.VMEM((CHUNKS, GROUPS - 1, CAP * CHUNK, features), bf16),
            pltpu.VMEM((CHUNKS, GROUPS, CAP * CHUNK, features), bf16),
            pltpu.VMEM((SHARDS, PAIR, features), bf16),
            pltpu.VMEM((SHARDS, PAIR, features), bf16),
            pltpu.VMEM((SHARDS, PAIR, features), bf16),
            held(2),
            held(GROUPS - 1),
            held(GROUPS - 1),
            small,
            small,
            small,
            small,
            pltpu.VMEM((SHARDS * PAIR, LANES), f32),
            dma((3,)),
            dma,
            dma((CHUNKS,)),
            dma,
            dma((CHUNKS,)),
            dma((2,)),
            dma((2,)),
            dma((2,)),
            dma((2,)),
        ],
        compiler_params=pltpu.CompilerParams(
            collective_id=0, has_side_effects=True, vmem_limit_bytes=63 * 2**20
        ),
        name="dedup",
    )(embeddings, cluster_id.reshape(1, rows), row_targets.T)
    return out.reshape(rows)


def solution(mesh):
    placed = (P(("shard", "grp"), None), P(("shard", "grp")), P(("shard", "grp"), None))
    return jax.shard_map(
        body, mesh=mesh, in_specs=placed, out_specs=P(("shard", "grp")), check_vma=False
    )
```

```python
import jax
import jax.numpy as jnp
from jax import lax
from jax.experimental import pallas as pl
from jax.experimental.pallas import tpu as pltpu
from jax.sharding import PartitionSpec as P

MESH = pl.DeviceIdType.MESH
SIDE = 8
CORES = 2
SHARDS = SIDE * SIDE * CORES
GROUPS = 4
CAP = 2
PAIR = GROUPS * CAP
LANES = 128
PLANE = SHARDS // CORES
LINES = GROUPS * CORES
CHUNK = 16
CHUNKS = SHARDS // CHUNK
ORDER = (4, 5, 0, 1, 2, 3, 6, 7)
EARLY = 2
TAGS_AFTER = 5
SCORED = (0, 32, 64, 96, 112, 128)


def sway(n):
    return (n + 1) // 2 * (n % 2 * 2 - 1) % SIDE


def steps(place):
    half = SIDE // 2
    chunk, pair, odd = place // CHUNK, place % CHUNK // 2, place % 2
    first = (chunk // CORES == 0) * 1
    sign = 1 - 2 * odd
    near, far = pair % half, pair // half
    dy = first * (sign * near + half * odd * ((near == 0) * 1)) + (1 - first) * sign * sway(pair)
    dz = dy + first * half * far + (1 - first) * sign * (chunk // CORES)
    return (dy + SIDE) % SIDE, (dz + 2 * SIDE) % SIDE, chunk % CORES


def shard_at(me, place, sign):
    dy, dz, dc = steps(place)
    y = (me // (SIDE * CORES) + sign * dy + SIDE) % SIDE
    z = ((me // CORES) % SIDE + sign * dz + SIDE) % SIDE
    c = (me + dc) % CORES
    return (y * SIDE + z) * CORES + c


def kernel(
    emb_hbm,
    cid_hbm,
    tgt_hbm,
    out_ref,
    emb_ref,
    cid_ref,
    tgt_ref,
    unit,
    hot,
    xsend,
    stage,
    ysend,
    recv,
    mid,
    tiles,
    tag_xs,
    ret_xs,
    tag_send,
    tag_recv,
    ret_send,
    ret_recv,
    peak,
    in_sem,
    xs_sem,
    xr_sem,
    ys_sem,
    yr_sem,
    tile_ss,
    tile_rs,
    row_ss,
    row_rs,
):
    rows, features = emb_ref.shape
    me = lax.axis_index("shard")
    grp = lax.axis_index("grp")
    f32 = jnp.float32
    bf16 = jnp.bfloat16

    incoming = [
        pltpu.make_async_copy(src, dst, in_sem.at[n])
        for n, (src, dst) in enumerate(
            [(tgt_hbm, tgt_ref), (cid_hbm, cid_ref), (emb_hbm, emb_ref)]
        )
    ]
    for copy in incoming:
        copy.start()

    ys = [(me // (SIDE * CORES) + d) % SIDE * (SIDE * CORES) for d in range(SIDE)]
    zs = [(me // CORES + d) % SIDE * CORES for d in range(SIDE)]
    cs = [(me + d) % CORES for d in range(CORES)]

    def at(dy, dz, dc):
        return {"shard": ys[dy % SIDE] + zs[dz % SIDE] + cs[dc]}

    def ahead(place):
        return at(*steps(place))

    def along(e, dc=0):
        return {"shard": ys[0] + zs[0] + cs[dc], "grp": (grp + e + GROUPS) % GROUPS}

    barrier = pltpu.get_barrier_semaphore()
    for e in range(1, GROUPS):
        for dc in range(CORES):
            pl.semaphore_signal(barrier, inc=1, device_id=along(e, dc), device_id_type=MESH)
    for place in range(1, SHARDS):
        pl.semaphore_signal(barrier, inc=1, device_id=ahead(place), device_id_type=MESH)

    place = lax.broadcasted_iota(jnp.int32, (SHARDS, 1), 0)
    peers = shard_at(me, place, 1) * GROUPS
    before = lax.broadcasted_iota(jnp.int32, (rows, rows), 0) < lax.broadcasted_iota(
        jnp.int32, (rows, rows), 1
    )
    before = jnp.where(before, 1.0, 0.0).astype(bf16)
    incoming[0].wait()
    named = []
    for e in range(GROUPS):
        target = peers + (grp + e) % GROUPS
        hit = tgt_ref[0:1, :] == target
        for c in range(1, tgt_ref.shape[0]):
            hit = hit | (tgt_ref[c : c + 1, :] == target)
        named.append(jnp.where(hit, 1.0, 0.0).astype(f32))
    named = jnp.concatenate(named, axis=0)
    rank = jnp.dot(named.astype(bf16), before, preferred_element_type=f32)
    for r in range(CAP):
        pick = jnp.where(rank == float(r), named, 0.0).astype(bf16)
        for e in range(GROUPS):
            hot[e * CAP + r] = pick[e * SHARDS : (e + 1) * SHARDS, :]

    incoming[2].wait()
    values = emb_ref[...].astype(f32)
    squares = jnp.sum(values * values, axis=1, keepdims=True)
    unit[...] = (values * lax.rsqrt(squares + 1e-06)).astype(bf16)

    size = PAIR * CHUNK
    order_out = lax.broadcasted_iota(jnp.int32, (size, size), 0)
    order_in = lax.broadcasted_iota(jnp.int32, (size, size), 1)
    turn = (order_in % CHUNK == order_out // PAIR) & (order_in // CHUNK == order_out % PAIR)
    turn = jnp.where(turn, 1.0, 0.0).astype(bf16)
    back = (order_out % CHUNK == order_in // PAIR) & (order_out // CHUNK == order_in % PAIR)
    back = jnp.where(back, 1.0, 0.0).astype(bf16)

    def by_place_first(block):
        block = jnp.dot(turn, block, preferred_element_type=f32).astype(bf16)
        return block.reshape(CHUNK, PAIR, features)

    def keep_for_x(k, j, block):
        e, r = j // CAP, j % CAP
        if e == 0:
            stage[k, 0, r * CHUNK : (r + 1) * CHUNK, :] = block
        else:
            xsend[k, e - 1, r * CHUNK : (r + 1) * CHUNK, :] = block

    def pack_rows(chunks):
        pick = [hot[j, k * CHUNK : (k + 1) * CHUNK, :] for k in chunks for j in range(PAIR)]
        packed = jnp.dot(
            jnp.concatenate(pick, axis=0), unit[...], preferred_element_type=f32
        ).astype(bf16)
        for n, k in enumerate(chunks):
            block = packed[n * size : (n + 1) * size, :]
            if k in ORDER[:EARLY]:
                ysend[k * CHUNK : (k + 1) * CHUNK] = by_place_first(block)
            else:
                for j in range(PAIR):
                    keep_for_x(k, j, block[j * CHUNK : (j + 1) * CHUNK, :])

    def x_copies(k):
        return [
            pltpu.make_async_remote_copy(
                src_ref=xsend.at[k, e - 1, pl.ds(r * CHUNK, CHUNK)],
                dst_ref=stage.at[k, e, pl.ds(r * CHUNK, CHUNK)],
                send_sem=xs_sem,
                recv_sem=xr_sem.at[k],
                device_id=along(e),
                device_id_type=MESH,
            )
            for r in range(CAP)
            for e in (1, 3, 2)
        ]

    def x_arrived(k):
        part = stage.at[k, pl.ds(1, GROUPS - 1)]
        pltpu.make_async_copy(part, part, xr_sem.at[k]).wait()
        return by_place_first(stage[k].reshape(size, features))

    def yz_arrived(k):
        first = max(1, k * CHUNK)
        part = pl.ds(first, (k + 1) * CHUNK - first)
        part = (mid if k in ORDER[:EARLY] else recv).at[part]
        pltpu.make_async_copy(part, part, yr_sem.at[k]).wait()

    def send_rows(n):
        k = ORDER[n]
        copies = [
            pltpu.make_async_remote_copy(
                src_ref=ysend.at[place],
                dst_ref=(mid if k in ORDER[:EARLY] else recv).at[place],
                send_sem=ys_sem,
                recv_sem=yr_sem.at[k],
                device_id=ahead(place),
                device_id_type=MESH,
            )
            for place in range(max(1, k * CHUNK), (k + 1) * CHUNK)
        ]
        if n + EARLY < CHUNKS:
            between = x_copies(ORDER[n + EARLY])
            for m, copy in enumerate(between):
                copies.insert(m + (m + 1) * CHUNK // (len(between) + 1), copy)
        for copy in copies:
            copy.start()

    def pass_rows(n):
        k = ORDER[n]
        ysend[k * CHUNK : (k + 1) * CHUNK] = x_arrived(k)
        if k == 0:
            recv[0] = ysend[0]
        send_rows(n)

    def turn_rows(k):
        yz_arrived(k)
        block = mid[k * CHUNK : (k + 1) * CHUNK].reshape(size, features)
        block = jnp.dot(back, block, preferred_element_type=f32).astype(bf16)
        for j in range(PAIR):
            keep_for_x(k, j, block[j * CHUNK : (j + 1) * CHUNK, :])
        for copy in x_copies(k):
            copy.start()

    pack_rows(ORDER[: 2 * EARLY])
    pl.semaphore_wait(barrier, SHARDS - 1 + (GROUPS - 1) * CORES)
    for n in range(EARLY):
        send_rows(n)
    pack_rows(ORDER[2 * EARLY :])

    def both_cores(block):
        block = [
            jnp.maximum(block[k * CHUNK : (k + 1) * CHUNK, :], block[(k + 1) * CHUNK : (k + 2) * CHUNK, :])
            for k in range(0, CHUNKS, CORES)
        ]
        return jnp.concatenate(block, axis=0)

    def spread_lines(n, plane, held, sign):
        missing = jnp.zeros((LANES - PLANE, LANES), f32)
        turned = jnp.transpose(jnp.concatenate([plane, missing], axis=0))
        for m in range(LINES):
            tiles[n, m] = turned[m * CAP : (m + 1) * CAP, :]
        for m in range(1, LINES):
            pltpu.make_async_remote_copy(
                src_ref=tiles.at[n, m],
                dst_ref=held.at[m - 1],
                send_sem=tile_ss.at[n],
                recv_sem=tile_rs.at[n],
                device_id=along(sign * (m % GROUPS), m // GROUPS),
                device_id_type=MESH,
            ).start()

    def merge_lines(n, held):
        pltpu.make_async_copy(held, held, tile_rs.at[n]).wait()
        line = lax.broadcasted_iota(jnp.int32, (LANES, LANES), 0)
        merged = jnp.zeros((LANES, LANES), f32)
        for m in range(LINES):
            lines = held[m - 1] if m else tiles[n, 0]
            for r in range(CAP):
                merged = jnp.where(line == m * CAP + r, lines[r : r + 1, :], merged)
        return jnp.transpose(merged)[0:PLANE, :]

    others = pl.ds(1, PLANE - 1)

    def spread_rows(n, sent, held, sign):
        held[0] = sent[0]
        for row in range(1, PLANE):
            dy, dz, _ = steps(row // CHUNK * CORES * CHUNK + row % CHUNK)
            pltpu.make_async_remote_copy(
                src_ref=sent.at[row],
                dst_ref=held.at[row],
                send_sem=row_ss.at[n],
                recv_sem=row_rs.at[n],
                device_id=at(sign * dy, sign * dz, 0),
                device_id_type=MESH,
            ).start()

    def rows_arrived(n, held):
        pltpu.make_async_copy(held.at[others], held.at[others], row_rs.at[n]).wait()

    incoming[1].wait()
    cid = cid_ref[...].astype(f32) + 1.0
    lane = lax.broadcasted_iota(jnp.int32, (SHARDS, LANES), 1)
    core_lane = lax.broadcasted_iota(jnp.int32, (SHARDS, LANES), 0) // CHUNK % CORES * PAIR
    tags = jnp.zeros((SHARDS, LANES), f32)
    for j in range(PAIR):
        tag = jnp.sum(hot[j].astype(f32) * cid, axis=1, keepdims=True)
        tags = jnp.where(lane == core_lane + j, tag, tags)
    spread_lines(0, both_cores(tags) - 1.0, tag_xs, 1)

    total = SHARDS * PAIR
    lanes = lax.broadcasted_iota(jnp.int32, (total, LANES), 1)
    member = lax.broadcasted_iota(jnp.int32, (total, LANES), 0)
    mine = lanes == member // (CHUNK * PAIR) % CORES * PAIR + member % PAIR
    number = lax.broadcasted_iota(jnp.int32, (total, 1), 0)
    column = lax.broadcasted_iota(jnp.int32, (1, total), 1)

    def member_tags():
        rows_arrived(0, tag_recv)
        spread = jnp.broadcast_to(tag_recv[...], (PLANE, PAIR, LANES)).reshape(PLANE * PAIR, LANES)
        block = CHUNK * PAIR
        spread = [spread[k // CORES * block : (k // CORES + 1) * block, :] for k in range(CHUNKS)]
        spread = jnp.concatenate(spread, axis=0)
        tag_col = jnp.sum(jnp.where(mine, spread, 0.0), axis=1, keepdims=True)
        tag_col = jnp.where(tag_col < 0.0, -2.0 - number.astype(f32), tag_col)
        return tag_col, jnp.transpose(jnp.broadcast_to(tag_col, (total, LANES)))[0:1, :]

    def fold(scores):
        best = scores[:, 0:LANES]
        for first in range(LANES, scores.shape[1], LANES):
            best = jnp.maximum(best, scores[:, first : first + LANES])
        return best

    def score(begin, end):
        for k in range(begin // CHUNK, end // CHUNK):
            if k in ORDER[:EARLY]:
                recv[k * CHUNK : (k + 1) * CHUNK] = x_arrived(k)
            else:
                yz_arrived(k)
        low, high = begin * PAIR, end * PAIR
        scores = lax.dot_general(
            recv[0:end].reshape(high, features),
            recv[begin:end].reshape(high - low, features),
            (((1,), (1,)), ((), ())),
            preferred_element_type=f32,
        )
        scores = jnp.where(tag_col[0:high, :] == tag_row[:, low:high], scores, -1.0)
        own = scores[low:high, :]
        own = fold(jnp.where(number[low:high, :] != column[:, low:high], own, -1.0))
        if low:
            past = scores[0:low, :]
            peak[0:low, :] = jnp.maximum(peak[0:low, :], fold(past))
            past = jnp.max(past, axis=0, keepdims=True)
            past = jnp.transpose(jnp.broadcast_to(past, (LANES, high - low)))
            own = jnp.maximum(own, past)
        peak[low:high, :] = own

    for n in range(EARLY, CHUNKS):
        pass_rows(n)
        if n == TAGS_AFTER:
            tag_send[...] = merge_lines(0, tag_xs).reshape(PLANE, 1, LANES)
            spread_rows(0, tag_send, tag_recv, 1)
    for n in range(EARLY):
        turn_rows(ORDER[n])
    tag_col, tag_row = member_tags()
    for begin, end in zip(SCORED[:-1], SCORED[1:]):
        score(begin, end)
    best = jnp.max(peak[...], axis=1, keepdims=True)
    best = jnp.where(mine, best, -2.0)
    best = both_cores(jnp.max(best.reshape(SHARDS, PAIR, LANES), axis=1))
    ret_send[...] = best.reshape(PLANE, 1, LANES)

    spread_rows(1, ret_send, ret_recv, -1)
    rows_arrived(1, ret_recv)
    spread_lines(1, ret_recv[...].reshape(PLANE, LANES), ret_xs, -1)
    final = merge_lines(1, ret_xs)
    final = jnp.concatenate(
        [
            final[k // CORES * CHUNK : (k // CORES + 1) * CHUNK, k % CORES * PAIR : (k % CORES + 1) * PAIR]
            for k in range(CHUNKS)
        ],
        axis=0,
    )
    found = jnp.full((SHARDS, rows), -1.0, f32)
    for j in range(PAIR):
        found = jnp.maximum(found, jnp.where(hot[j] > 0.5, final[:, j : j + 1], -1.0))
    out_ref[...] = jnp.max(found, axis=0, keepdims=True)

    pltpu.make_async_copy(xsend, xsend, xs_sem).wait()
    part = ysend.at[pl.ds(1, SHARDS - 1)]
    pltpu.make_async_copy(part, part, ys_sem).wait()
    for n, held in enumerate((tag_xs, ret_xs)):
        pltpu.make_async_copy(held, held, tile_ss.at[n]).wait()
    for n, sent in enumerate((tag_send, ret_send)):
        pltpu.make_async_copy(sent.at[others], sent.at[others], row_ss.at[n]).wait()


def body(embeddings, cluster_id, row_targets):
    rows = embeddings.shape[0]
    features = embeddings.shape[1]
    copies = row_targets.shape[1]
    f32, bf16 = jnp.float32, jnp.bfloat16
    dma = pltpu.SemaphoreType.DMA

    held = pltpu.VMEM((LINES - 1, CAP, LANES), f32)
    small = pltpu.VMEM((PLANE, 1, LANES), f32)
    out = pl.pallas_call(
        kernel,
        out_shape=jax.ShapeDtypeStruct((1, rows), f32),
        in_specs=[pl.BlockSpec(memory_space=pltpu.HBM)] * 3,
        out_specs=pl.BlockSpec(memory_space=pltpu.VMEM),
        scratch_shapes=[
            pltpu.VMEM((rows, features), bf16),
            pltpu.VMEM((1, rows), jnp.int32),
            pltpu.VMEM((copies, rows), jnp.int32),
            pltpu.VMEM((rows, features), bf16),
            pltpu.VMEM((PAIR, SHARDS, rows), bf16),
            pltpu.VMEM((CHUNKS, GROUPS - 1, CAP * CHUNK, features), bf16),
            pltpu.VMEM((CHUNKS, GROUPS, CAP * CHUNK, features), bf16),
            pltpu.VMEM((SHARDS, PAIR, features), bf16),
            pltpu.VMEM((SHARDS, PAIR, features), bf16),
            pltpu.VMEM((SHARDS, PAIR, features), bf16),
            pltpu.VMEM((2, LINES, CAP, LANES), f32),
            held,
            held,
            small,
            small,
            small,
            small,
            pltpu.VMEM((SHARDS * PAIR, LANES), f32),
            dma((3,)),
            dma,
            dma((CHUNKS,)),
            dma,
            dma((CHUNKS,)),
            dma((2,)),
            dma((2,)),
            dma((2,)),
            dma((2,)),
        ],
        compiler_params=pltpu.CompilerParams(
            collective_id=0, has_side_effects=True, vmem_limit_bytes=63 * 2**20
        ),
        name="dedup",
    )(embeddings, cluster_id.reshape(1, rows), row_targets.T)
    return out.reshape(rows)


def solution(mesh):
    placed = (P(("shard", "grp"), None), P(("shard", "grp")), P(("shard", "grp"), None))
    return jax.shard_map(
        body, mesh=mesh, in_specs=placed, out_specs=P(("shard", "grp")), check_vma=False
    )
```
